128 devices in a mesh: kv: 32 (over z, x, core), tp: 4 (over y).
Axes of the slice: x: 4, y: 4, z: 4, core: 2. Of those that a mesh axis runs over, the one named last changes fastest.
Arguments:
- query: bfloat16 [4, 128, 128], P(None, 'tp'), may hold values from -8 to 28
- key_cache: bfloat16 [8192, 16, 8, 128], P('kv', None, 'tp'), may hold values from -6 to 7
- value_cache: bfloat16 [8192, 16, 8, 128], P('kv', None, 'tp'), may hold values from -6 to 6
- seq_lengths: int32 [4], replicated, may hold values from 1 to 32768, as said below
- block_table: int32 [4, 2048], P(None, 'kv'), may hold values from 0 to 255, as said below
- residual: bfloat16 [4, 16384], replicated, may hold values from -6 to 6
- norm_gain: bfloat16 [16384], replicated, may hold values from 0.099609375 to 1.8984375
- gate_weight: bfloat16 [26624, 16384], P(('kv', 'tp')), may hold values from -0.046875 to 0.046875
- up_weight: bfloat16 [26624, 16384], P(('kv', 'tp')), may hold values from -0.046875 to 0.046875
- down_weight: bfloat16 [26624, 16384], P(('kv', 'tp')), may hold values from -0.125 to 0.125
Outputs:
- layer_out: bfloat16 [4, 16384], P(None, ('kv', 'tp'))
- attention: bfloat16 [4, 128, 128], P(None, 'tp')
The draws below stay inside these ranges and needn't reach their ends.
Inputs may be any that keep to these rules, and one draw needn't show every extreme that they name: `seq_lengths`: each sequence has at least one live position; some sequence has all 32768 positions live. `block_table`: for each index of kv, the columns of its 64 logical blocks hold, over all rows together, every page number once.
All inputs are finite; a program needn't handle non-finite values.
Results may differ from the reference program's by a relative error of at most 0.01.
Values may be sent and summed in bfloat16 or wider, within the bound.
No kernel may reach another device: no remote copies, remote signals or barrier semaphores. Data moves between devices by JAX's collectives and lax.ppermute only.
A program may use at most 128 MiB of HBM per device.

```python
import jax
import jax.numpy as jnp
from jax import lax

ROWS = 4
PAGE = 16
NH = 128
KVH = 8
HD = 128
FF = 26624
QPK = 16
D = 16384
LENGTH = 32768
BPD = 64
PAGES_DEV = 256
PAGES = 8192
N_KV = 32


def draw_query(key, part):
    key = jax.random.fold_in(key, 11)
    base = jax.random.normal(key, (ROWS, NH, HD), jnp.float32)
    return jnp.clip(2.0 * base, -8.0, 8.0).astype(jnp.bfloat16)


def draw_key_cache(key, part):
    key = jax.random.fold_in(key, 12)
    base = jax.random.normal(key, (PAGES, PAGE, KVH, HD), jnp.float32)
    return jnp.clip(base, -6.0, 6.0).astype(jnp.bfloat16)


def draw_seq_lengths(key, part):
    key = jax.random.fold_in(key, 13)
    values = jax.random.randint(key, (ROWS,), 1, LENGTH + 1, jnp.int32)
    chosen = jax.random.randint(jax.random.fold_in(key, 1), (), 0, ROWS, jnp.int32)
    return jnp.where(jnp.arange(ROWS, dtype=jnp.int32) == chosen, LENGTH, values).astype(jnp.int32)


def draw_block_table(key, part):
    key = jax.random.fold_in(key, 14)
    device_keys = jax.random.split(key, N_KV)
    orders = jax.vmap(lambda single: jax.random.permutation(single, PAGES_DEV))(device_keys)
    arranged = orders.reshape(N_KV, ROWS, BPD).transpose(1, 0, 2)
    return arranged.reshape(ROWS, N_KV * BPD).astype(jnp.int32)


def strengthened(result, stream_key, source, target, parts, factor):
    def block_of(dim):
        return (jnp.arange(result.shape[dim]) // (result.shape[dim] // parts)).reshape((-1,) + (1,) * (result.ndim - 1 - dim))

    first = jax.random.permutation(stream_key, parts)[block_of(target)]
    second = (block_of(target) + parts // 2) % parts
    return jnp.where((block_of(source) == first) | (block_of(source) == second), factor * result, result)


def levels(rng, extent, shards, smallest, high):
    gain, own = 1.0, jax.random.fold_in(rng, 6)
    for axis_at, shards_of in shards:
        steps = jnp.exp(jax.random.uniform(jax.random.fold_in(own, axis_at), (shards_of,), jnp.float32, smallest / len(shards), high / len(shards)))
        gain = gain * jnp.repeat(steps, extent[axis_at] // shards_of).reshape([-1 if axis == axis_at else 1 for axis in range(len(extent))])
    return gain


def scatter_about(stream_key, shape, width, bound, cuts=(), kind=jnp.bfloat16):
    drawn = width * jax.random.normal(stream_key, shape, jnp.float32)
    if cuts:
        drawn = drawn * levels(stream_key, shape, cuts, -0.22, 0.18)
    return jnp.clip(drawn, -bound, bound).astype(kind)


def heavy_noise(rng, shape, scale, reach, cuts, heavy, held_as=jnp.bfloat16):
    result = scale * jax.random.normal(rng, shape, jnp.float32)
    if cuts:
        result = result * levels(rng, shape, cuts, -0.22, 0.18)
    return jnp.clip(strengthened(result, jax.random.fold_in(rng, 3), *heavy), -reach, reach).astype(held_as)


def setup_inputs(seed: int = 0) -> dict:
    key_list = jax.random.split(jax.random.key(seed), 11)
    query = draw_query(jax.random.fold_in(key_list[10], 71), 0)
    key_cache = draw_key_cache(jax.random.fold_in(key_list[10], 71), 0)
    value_cache = scatter_about(key_list[2], (PAGES, PAGE, KVH, HD), 1.0, 6.0, ((0, 32), (2, 4)))
    seq_lengths = draw_seq_lengths(jax.random.fold_in(key_list[10], 71), 0)
    block_table = draw_block_table(jax.random.fold_in(key_list[10], 71), 0)
    residual = scatter_about(key_list[5], (ROWS, D), 1.0, 6.0)
    norm_gain = jnp.clip(1.0 + 0.18 * jax.random.normal(key_list[6], (D,), jnp.float32), 0.099609375, 1.8984375).astype(jnp.bfloat16)
    gate_weight = scatter_about(key_list[7], (FF, D), D ** -0.5, 0.046875, ((0, 128),))
    up_weight = scatter_about(key_list[8], (FF, D), D ** -0.5, 0.046875, ((0, 128),))
    down_weight = heavy_noise(key_list[9], (FF, D), FF ** -0.5, 0.125, ((0, 128),), (0, 1, 128, 5.5))
    return {"query": query, "key_cache": key_cache, "value_cache": value_cache, "seq_lengths": seq_lengths, "block_table": block_table, "residual": residual, "norm_gain": norm_gain, "gate_weight": gate_weight, "up_weight": up_weight, "down_weight": down_weight}


NEG = -1e+30

def row_attention(query_row, table_row, length_row, key_cache, value_cache):
    block_count = table_row.shape[0]
    holder = jnp.arange(block_count, dtype=jnp.int32) // BPD
    page_index = (holder * PAGES_DEV + table_row).astype(jnp.int32)
    keys_row = key_cache[page_index].reshape(LENGTH, KVH, HD).astype(jnp.float32)
    values_row = value_cache[page_index].reshape(LENGTH, KVH, HD).astype(jnp.float32)
    grouped = query_row.astype(jnp.float32).reshape(KVH, QPK, HD)
    scores = jnp.einsum('gqd,cgd->gqc', grouped, keys_row) * HD ** (-0.5)
    active = (jnp.arange(LENGTH, dtype=jnp.int32) < length_row)[None, None, :]
    masked = jnp.where(active, scores, NEG)
    top_score = lax.optimization_barrier(jnp.max(masked, axis=-1, keepdims=True))
    weights = jnp.where(active, jnp.exp(masked - top_score), 0.0)
    denominator = lax.optimization_barrier(jnp.sum(weights, axis=-1))
    rounded = weights.astype(jnp.bfloat16).astype(jnp.float32)
    summed = jnp.einsum('gqc,cgd->gqd', rounded, values_row)
    return (summed / denominator[..., None]).reshape(NH, HD).astype(jnp.bfloat16)

def reference(query, key_cache, value_cache, seq_lengths, block_table, residual, norm_gain, gate_weight, up_weight, down_weight):

    def one_row(packed):
        query_row, table_row, length_row = packed
        return row_attention(query_row, table_row, length_row, key_cache, value_cache)
    attention = lax.map(one_row, (query, block_table, seq_lengths))
    hidden_state = residual.astype(jnp.float32) + attention.reshape(ROWS, D).astype(jnp.float32)
    mean_square = lax.optimization_barrier(jnp.mean(hidden_state * hidden_state, axis=-1, keepdims=True))
    normed = (hidden_state * lax.rsqrt(mean_square + 1e-05) * norm_gain.astype(jnp.float32)).astype(jnp.bfloat16)
    gate_value = jnp.dot(normed, gate_weight.T, preferred_element_type=jnp.float32)
    up_value = jnp.dot(normed, up_weight.T, preferred_element_type=jnp.float32)
    activated = (jax.nn.silu(gate_value) * up_value).astype(jnp.bfloat16)
    mixed = jnp.dot(activated, down_weight, preferred_element_type=jnp.float32)
    return ((hidden_state + mixed).astype(jnp.bfloat16), attention)
```

```python
import functools

import jax
import jax.numpy as jnp
from jax import lax
from jax.experimental import pallas as pl
from jax.experimental.pallas import tpu as pltpu
from jax.sharding import PartitionSpec as P

NEG = -1e30
F32 = jnp.float32
BF16 = jnp.bfloat16
MIB = 1 << 20
NT = (((1,), (1,)), ((), ()))
PAGES_PER_DOT = 8


def attention_kernel(lengths, table, query, keys, values, out, k_vmem, v_vmem, sems):
    rows, heads, width = query.shape
    pages = table.shape[1]
    cells = keys.shape[0] // (rows * pages)
    k_copy = pltpu.make_async_copy(keys, k_vmem, sems.at[0])
    v_copy = pltpu.make_async_copy(values, v_vmem, sems.at[1])
    k_copy.start()
    v_copy.start()
    first = lax.axis_index("kv") * (pages * cells // 2)
    span = pages * cells
    column = lax.broadcasted_iota(jnp.int32, (heads, span), 1)
    head = lax.broadcasted_iota(jnp.int32, (heads, span), 0)
    own = (column % 2) == (head // (heads // 2))
    position = jnp.where(own, first + column // 2, jnp.int32(2**30))
    lane = lax.broadcasted_iota(jnp.int32, (heads, width), 1)

    def block(ref, row, at):
        return jnp.concatenate(
            [
                ref[pl.ds(pl.multiple_of(table[row, at + i] * cells, cells), cells), :]
                for i in range(PAGES_PER_DOT)
            ],
            axis=0,
        )

    kept = []
    k_copy.wait()
    for row in range(rows):
        q = query[row]
        scores = jnp.concatenate(
            [
                lax.dot_general(q, block(k_vmem, row, at), NT, preferred_element_type=F32)
                for at in range(0, pages, PAGES_PER_DOT)
            ],
            axis=1,
        ) * (width**-0.5)
        active = position < lengths[row]
        masked = jnp.where(active, scores, NEG)
        top = jnp.max(masked, axis=-1, keepdims=True)
        weights = jnp.where(active, jnp.exp(masked - top), 0.0)
        total = jnp.sum(weights, axis=-1, keepdims=True)
        kept.append(weights.astype(BF16))
        out[:, rows + row, :] = jnp.where(lane < width // 2, top, total)
    v_copy.wait()
    for row in range(rows):
        summed = jnp.zeros((heads, width), F32)
        for at in range(0, pages, PAGES_PER_DOT):
            summed += jnp.dot(
                kept[row][:, at * cells : (at + PAGES_PER_DOT) * cells],
                block(v_vmem, row, at),
                preferred_element_type=F32,
            )
        out[:, row, :] = summed


def merge_kernel(parts, out):
    count, double, width = parts.shape
    rows = double // 2
    stats = parts[:, rows:, :]
    top = stats[:, :, 0:1]
    total = stats[:, :, width // 2 : width // 2 + 1]
    highest = jnp.max(top, axis=0, keepdims=True)
    factor = jnp.exp(top - highest)
    denominator = jnp.sum(factor * total, axis=0)
    summed = jnp.sum(factor * parts[:, :rows, :], axis=0)
    done = (summed / denominator).astype(BF16)
    out[...] = jnp.broadcast_to(done[None], out.shape)


def feed_kernel(heads, residual, gain, gate_w, up_w, down_w, out, normed, chunk):
    count, rows, width = heads.shape
    features = count * width
    squares = jnp.zeros((rows, width), F32)
    for i in range(count):
        cols = slice(i * width, (i + 1) * width)
        hidden = residual[:, cols].astype(F32) + heads[i].astype(F32)
        squares += hidden * hidden
    mean_square = jnp.sum(squares, axis=-1, keepdims=True) / features
    scale = lax.rsqrt(mean_square + 1e-05)
    for i in range(count):
        cols = slice(i * width, (i + 1) * width)
        hidden = residual[:, cols].astype(F32) + heads[i].astype(F32)
        normed[:, cols] = (hidden * scale * gain[:, cols].astype(F32)).astype(BF16)
    units = gate_w.shape[0]
    gate = jnp.zeros((rows, units), F32)
    up = jnp.zeros((rows, units), F32)
    for at in range(0, features, chunk):
        x = normed[:, at : at + chunk]
        gate += lax.dot_general(x, gate_w[:, at : at + chunk], NT, preferred_element_type=F32)
        up += lax.dot_general(x, up_w[:, at : at + chunk], NT, preferred_element_type=F32)
    activated = (gate / (1.0 + jnp.exp(-gate)) * up).astype(BF16)
    for at in range(0, features, chunk):
        mixed = jnp.dot(activated, down_w[:, at : at + chunk], preferred_element_type=F32)
        for j in range(chunk // width):
            out[at // width + j] = mixed[:, j * width : (j + 1) * width]


def final_kernel(parts, heads, residual, out):
    count, rows, width = parts.shape
    share = lax.axis_index("kv") * lax.axis_size("tp") + lax.axis_index("tp")
    cols = pl.ds(pl.multiple_of(share * width, width), width)
    hidden = residual[:, cols].astype(F32) + heads[share].astype(F32)
    out[...] = (hidden + jnp.sum(parts[...], axis=0)).astype(BF16)


VMEM = pl.BlockSpec(memory_space=pltpu.VMEM)
SMEM = pl.BlockSpec(memory_space=pltpu.SMEM)
ANY = pl.BlockSpec(memory_space=pl.ANY)


def in_vmem(x):
    return pltpu.with_memory_space_constraint(x, pltpu.VMEM)


def shards(
    query,
    key_cache,
    value_cache,
    seq_lengths,
    block_table,
    residual,
    norm_gain,
    gate_weight,
    up_weight,
    down_weight,
):
    rows, heads, width = query.shape
    keys = key_cache.reshape(-1, width)
    values = value_cache.reshape(-1, width)
    kv_size, tp_size = lax.axis_size("kv"), lax.axis_size("tp")
    devices = kv_size * tp_size
    partials = pl.pallas_call(
        attention_kernel,
        out_shape=jax.ShapeDtypeStruct((heads, 2 * rows, width), F32),
        in_specs=[SMEM, SMEM, VMEM, ANY, ANY],
        out_specs=VMEM,
        scratch_shapes=[
            pltpu.VMEM(keys.shape, BF16),
            pltpu.VMEM(values.shape, BF16),
            pltpu.SemaphoreType.DMA((2,)),
        ],
        compiler_params=pltpu.CompilerParams(vmem_limit_bytes=16 * MIB),
        name="attention_partials",
    )(seq_lengths, block_table, query, keys, values)
    gathered = lax.all_to_all(partials, "kv", 0, 0, tiled=True)
    finished = pl.pallas_call(
        merge_kernel,
        out_shape=jax.ShapeDtypeStruct((devices, rows, width), BF16),
        in_specs=[VMEM],
        out_specs=VMEM,
        compiler_params=pltpu.CompilerParams(vmem_limit_bytes=16 * MIB),
        name="merge_blocks",
    )(gathered)
    all_heads = lax.all_to_all(finished, ("tp", "kv"), 0, 0, tiled=True)
    mixed = pl.pallas_call(
        functools.partial(feed_kernel, chunk=2048),
        out_shape=jax.ShapeDtypeStruct((devices, rows, width), F32),
        in_specs=[VMEM] * 6,
        out_specs=VMEM,
        scratch_shapes=[pltpu.VMEM((rows, devices * width), BF16)],
        compiler_params=pltpu.CompilerParams(vmem_limit_bytes=16 * MIB),
        name="feed_forward",
    )(
        all_heads,
        residual,
        norm_gain.reshape(1, -1),
        in_vmem(gate_weight),
        in_vmem(up_weight),
        in_vmem(down_weight),
    )
    sums = lax.all_to_all(mixed, ("kv", "tp"), 0, 0, tiled=True)
    layer_out = pl.pallas_call(
        final_kernel,
        out_shape=jax.ShapeDtypeStruct((rows, width), BF16),
        in_specs=[VMEM] * 3,
        out_specs=VMEM,
        compiler_params=pltpu.CompilerParams(vmem_limit_bytes=16 * MIB),
        name="add_shares",
    )(sums, all_heads, residual)
    own_heads = lax.dynamic_slice_in_dim(all_heads, lax.axis_index("tp") * heads, heads, 0)
    return layer_out, own_heads.transpose(1, 0, 2)


def solution(mesh):
    placed = (
        P(None, "tp", None),
        P("kv", None, "tp", None),
        P("kv", None, "tp", None),
        P(),
        P(None, "kv"),
        P(),
        P(),
        P(("kv", "tp"), None),
        P(("kv", "tp"), None),
        P(("kv", "tp"), None),
    )
    return jax.shard_map(
        shards,
        mesh=mesh,
        in_specs=placed,
        out_specs=(P(None, ("kv", "tp")), P(None, "tp", None)),
        check_vma=False,
    )
```

```python
import jax
import jax.numpy as jnp
from jax import lax
from jax.experimental import pallas as pl
from jax.experimental.pallas import tpu as pltpu
from jax.sharding import PartitionSpec as P

NEG = -1e30
F32 = jnp.float32
BF16 = jnp.bfloat16
MIB = 1 << 20
NT = (((1,), (1,)), ((), ()))
PAGES_PER_DOT = 8
PARTS = 4
CHUNK = 2048
IN_STEPS = 8
OUT_STEPS = 4


def attention_kernel(
    lengths_h, table_h, query_h, keys, values, out, lengths, table, query, k_vmem, v_vmem, sems
):
    rows, heads, width = query.shape
    pages = table.shape[1]
    cells = keys.shape[0] // (rows * pages)
    small = [
        pltpu.make_async_copy(table_h, table, sems.at[0]),
        pltpu.make_async_copy(lengths_h, lengths, sems.at[1]),
        pltpu.make_async_copy(query_h, query, sems.at[2]),
    ]
    part = keys.shape[0] // PARTS
    k_copies, v_copies = [], []
    for i in range(PARTS):
        at = pl.ds(i * part, part)
        k_copies.append(pltpu.make_async_copy(keys.at[at], k_vmem.at[at], sems.at[3 + i]))
        v_copies.append(pltpu.make_async_copy(values.at[at], v_vmem.at[at], sems.at[3 + PARTS + i]))
    for copy in small + k_copies + v_copies:
        copy.start()
    first = lax.axis_index("kv") * (pages * cells // 2)
    span = pages * cells
    column = lax.broadcasted_iota(jnp.int32, (heads, span), 1)
    head = lax.broadcasted_iota(jnp.int32, (heads, span), 0)
    own = (column % 2) == (head // (heads // 2))
    position = jnp.where(own, first + column // 2, jnp.int32(2**30))
    lane = lax.broadcasted_iota(jnp.int32, (heads, width), 1)

    def block(ref, row, at):
        return jnp.concatenate(
            [
                ref[pl.ds(pl.multiple_of(table[row, at + i] * cells, cells), cells), :]
                for i in range(PAGES_PER_DOT)
            ],
            axis=0,
        )

    kept = []
    for copy in small + k_copies:
        copy.wait()
    for row in range(rows):
        q = query[row]
        scores = jnp.concatenate(
            [
                lax.dot_general(q, block(k_vmem, row, at), NT, preferred_element_type=F32)
                for at in range(0, pages, PAGES_PER_DOT)
            ],
            axis=1,
        ) * (width**-0.5)
        active = position < lengths[row]
        masked = jnp.where(active, scores, NEG)
        top = jnp.max(masked, axis=-1, keepdims=True)
        weights = jnp.where(active, jnp.exp(masked - top), 0.0)
        total = jnp.sum(weights, axis=-1, keepdims=True)
        kept.append(weights.astype(BF16))
        out[:, rows + row, :] = jnp.where(lane < width // 2, top, total)
    for copy in v_copies:
        copy.wait()
    for row in range(rows):
        summed = jnp.zeros((heads, width), F32)
        for at in range(0, pages, PAGES_PER_DOT):
            summed += jnp.dot(
                kept[row][:, at * cells : (at + PAGES_PER_DOT) * cells],
                block(v_vmem, row, at),
                preferred_element_type=F32,
            )
        out[:, row, :] = summed


def merge_kernel(parts, out):
    count, double, width = parts.shape
    rows = double // 2
    stats = parts[:, rows:, :]
    top = stats[:, :, 0:1]
    total = stats[:, :, width // 2 : width // 2 + 1]
    highest = jnp.max(top, axis=0, keepdims=True)
    factor = jnp.exp(top - highest)
    denominator = jnp.sum(factor * total, axis=0)
    summed = jnp.sum(factor * parts[:, :rows, :], axis=0)
    done = (summed / denominator).astype(BF16)
    out[...] = jnp.broadcast_to(done[None], out.shape)


def feed_kernel(
    heads, residual_h, gain_h, gate_h, up_h, down_h, out, residual, gain, gate_w, up_w, down_w, normed, sems
):
    count, rows, width = heads.shape
    features = count * width
    small = [
        pltpu.make_async_copy(residual_h, residual, sems.at[3, 0]),
        pltpu.make_async_copy(gain_h, gain, sems.at[3, 1]),
    ]
    in_step = features // IN_STEPS
    out_step = features // OUT_STEPS

    def pieces(source, target, which, steps):
        step = features // steps
        copies = []
        for i in range(steps):
            at = pl.ds(i * step, step)
            copies.append(
                pltpu.make_async_copy(source.at[:, at], target.at[:, at], sems.at[which, i])
            )
        return copies

    gate_copies = pieces(gate_h, gate_w, 0, IN_STEPS)
    up_copies = pieces(up_h, up_w, 1, IN_STEPS)
    down_copies = pieces(down_h, down_w, 2, OUT_STEPS)
    for copy in small:
        copy.start()
    for i in range(IN_STEPS):
        gate_copies[i].start()
        up_copies[i].start()
    for copy in down_copies:
        copy.start()
    for copy in small:
        copy.wait()
    squares = jnp.zeros((rows, width), F32)
    for i in range(count):
        cols = slice(i * width, (i + 1) * width)
        hidden = residual[:, cols].astype(F32) + heads[i].astype(F32)
        squares += hidden * hidden
    mean_square = jnp.sum(squares, axis=-1, keepdims=True) / features
    scale = lax.rsqrt(mean_square + 1e-05)
    for i in range(count):
        cols = slice(i * width, (i + 1) * width)
        hidden = residual[:, cols].astype(F32) + heads[i].astype(F32)
        normed[:, cols] = (hidden * scale * gain[i : i + 1, :].astype(F32)).astype(BF16)
    units = gate_w.shape[0]
    gate = jnp.zeros((rows, units), F32)
    up = jnp.zeros((rows, units), F32)
    for i in range(IN_STEPS):
        at = i * in_step
        x = normed[:, at : at + in_step]
        gate_copies[i].wait()
        up_copies[i].wait()
        gate += lax.dot_general(x, gate_w[:, at : at + in_step], NT, preferred_element_type=F32)
        up += lax.dot_general(x, up_w[:, at : at + in_step], NT, preferred_element_type=F32)
    activated = (gate / (1.0 + jnp.exp(-gate)) * up).astype(BF16)
    for i in range(OUT_STEPS):
        at = i * out_step
        down_copies[i].wait()
        for half in range(at, at + out_step, CHUNK):
            mixed = jnp.dot(activated, down_w[:, half : half + CHUNK], preferred_element_type=F32)
            for j in range(CHUNK // width):
                out[half // width + j] = mixed[:, j * width : (j + 1) * width]


def final_kernel(parts, heads, residual, out):
    count, rows, width = parts.shape
    share = lax.axis_index("kv") * lax.axis_size("tp") + lax.axis_index("tp")
    cols = pl.ds(pl.multiple_of(share * width, width), width)
    hidden = residual[:, cols].astype(F32) + heads[share].astype(F32)
    out[...] = (hidden + jnp.sum(parts[...], axis=0)).astype(BF16)


VMEM = pl.BlockSpec(memory_space=pltpu.VMEM)
HBM = pl.BlockSpec(memory_space=pltpu.HBM)


def in_hbm(*arrays):
    return [pltpu.with_memory_space_constraint(x, pltpu.HBM) for x in arrays]


def shards(
    query,
    key_cache,
    value_cache,
    seq_lengths,
    block_table,
    residual,
    norm_gain,
    gate_weight,
    up_weight,
    down_weight,
):
    rows, heads, width = query.shape
    keys = key_cache.reshape(-1, width)
    values = value_cache.reshape(-1, width)
    kv_size, tp_size = lax.axis_size("kv"), lax.axis_size("tp")
    devices = kv_size * tp_size
    partials = pl.pallas_call(
        attention_kernel,
        out_shape=jax.ShapeDtypeStruct((heads, 2 * rows, width), F32),
        in_specs=[HBM] * 5,
        out_specs=VMEM,
        scratch_shapes=[
            pltpu.SMEM(seq_lengths.shape, jnp.int32),
            pltpu.SMEM(block_table.shape, jnp.int32),
            pltpu.VMEM(query.shape, BF16),
            pltpu.VMEM(keys.shape, BF16),
            pltpu.VMEM(values.shape, BF16),
            pltpu.SemaphoreType.DMA((3 + 2 * PARTS,)),
        ],
        compiler_params=pltpu.CompilerParams(vmem_limit_bytes=16 * MIB),
        name="attention_partials",
    )(*in_hbm(seq_lengths, block_table, query, keys, values))
    gathered = lax.all_to_all(partials, "kv", 0, 0, tiled=True)
    finished = pl.pallas_call(
        merge_kernel,
        out_shape=jax.ShapeDtypeStruct((devices, rows, width), BF16),
        in_specs=[VMEM],
        out_specs=VMEM,
        compiler_params=pltpu.CompilerParams(vmem_limit_bytes=16 * MIB),
        name="merge_blocks",
    )(gathered)
    all_heads = lax.all_to_all(finished, ("tp", "kv"), 0, 0, tiled=True)
    mixed = pl.pallas_call(
        feed_kernel,
        out_shape=jax.ShapeDtypeStruct((devices, rows, width), F32),
        in_specs=[VMEM] + [HBM] * 5,
        out_specs=VMEM,
        scratch_shapes=[
            pltpu.VMEM(residual.shape, BF16),
            pltpu.VMEM((devices, width), BF16),
            pltpu.VMEM(gate_weight.shape, BF16),
            pltpu.VMEM(up_weight.shape, BF16),
            pltpu.VMEM(down_weight.shape, BF16),
            pltpu.VMEM((rows, devices * width), BF16),
            pltpu.SemaphoreType.DMA((4, IN_STEPS)),
        ],
        compiler_params=pltpu.CompilerParams(vmem_limit_bytes=32 * MIB),
        name="feed_forward",
    )(
        all_heads,
        *in_hbm(residual, norm_gain.reshape(devices, width), gate_weight, up_weight, down_weight),
    )
    sums = lax.all_to_all(mixed, ("kv", "tp"), 0, 0, tiled=True)
    layer_out = pl.pallas_call(
        final_kernel,
        out_shape=jax.ShapeDtypeStruct((rows, width), BF16),
        in_specs=[VMEM] * 3,
        out_specs=VMEM,
        compiler_params=pltpu.CompilerParams(vmem_limit_bytes=16 * MIB),
        name="add_shares",
    )(sums, all_heads, residual)
    own_heads = lax.dynamic_slice_in_dim(all_heads, lax.axis_index("tp") * heads, heads, 0)
    return layer_out, own_heads.transpose(1, 0, 2)


def solution(mesh):
    placed = (
        P(None, "tp", None),
        P("kv", None, "tp", None),
        P("kv", None, "tp", None),
        P(),
        P(None, "kv"),
        P(),
        P(),
        P(("kv", "tp"), None),
        P(("kv", "tp"), None),
        P(("kv", "tp"), None),
    )
    return jax.shard_map(
        shards,
        mesh=mesh,
        in_specs=placed,
        out_specs=(P(None, ("kv", "tp")), P(None, "tp", None)),
        check_vma=False,
    )
```

```python
import functools

import jax
import jax.numpy as jnp
from jax import lax
from jax.experimental import pallas as pl
from jax.experimental.pallas import tpu as pltpu
from jax.sharding import Mesh
from jax.sharding import PartitionSpec as P

NEG = -1e30
F32 = jnp.float32
BF16 = jnp.bfloat16
MIB = 1 << 20
NT = (((1,), (1,)), ((), ()))
PAGES_PER_DOT = 8
PARTS = 4
CHUNK = 2048
IN_STEPS = 8
OUT_STEPS = 4


def kv_index():
    return lax.axis_index("chip") * lax.axis_size("core") + lax.axis_index("core")


def attention_kernel(
    lengths_h, table_h, query_h, keys, values, keep, send, lengths, table, query, k_vmem, v_vmem, sems
):
    rows, heads, width = query.shape
    pages = table.shape[1]
    cells = keys.shape[0] // (rows * pages)
    small = [
        pltpu.make_async_copy(table_h, table, sems.at[0]),
        pltpu.make_async_copy(lengths_h, lengths, sems.at[1]),
        pltpu.make_async_copy(query_h, query, sems.at[2]),
    ]
    part = keys.shape[0] // PARTS
    k_copies, v_copies = [], []
    for i in range(PARTS):
        at = pl.ds(i * part, part)
        k_copies.append(pltpu.make_async_copy(keys.at[at], k_vmem.at[at], sems.at[3 + i]))
        v_copies.append(pltpu.make_async_copy(values.at[at], v_vmem.at[at], sems.at[3 + PARTS + i]))
    for copy in small + k_copies + v_copies:
        copy.start()
    first = kv_index() * (pages * cells // 2)
    span = pages * cells
    column = lax.broadcasted_iota(jnp.int32, (heads, span), 1)
    head = lax.broadcasted_iota(jnp.int32, (heads, span), 0)
    own = (column % 2) == (head // (heads // 2))
    position = jnp.where(own, first + column // 2, jnp.int32(2**30))
    lane = lax.broadcasted_iota(jnp.int32, (heads, width), 1)
    half = heads // 2
    core = lax.axis_index("core")

    def put(row, block):
        low, high = block[:half], block[half:]
        keep[:, row, :] = jnp.where(core == 0, low, high)
        send[:, row, :] = jnp.where(core == 0, high, low)

    def block(ref, row, at):
        return jnp.concatenate(
            [
                ref[pl.ds(pl.multiple_of(table[row, at + i] * cells, cells), cells), :]
                for i in range(PAGES_PER_DOT)
            ],
            axis=0,
        )

    kept = []
    for copy in small + k_copies:
        copy.wait()
    for row in range(rows):
        q = query[row]
        scores = jnp.concatenate(
            [
                lax.dot_general(q, block(k_vmem, row, at), NT, preferred_element_type=F32)
                for at in range(0, pages, PAGES_PER_DOT)
            ],
            axis=1,
        ) * (width**-0.5)
        active = position < lengths[row]
        masked = jnp.where(active, scores, NEG)
        top = jnp.max(masked, axis=-1, keepdims=True)
        weights = jnp.where(active, jnp.exp(masked - top), 0.0)
        total = jnp.sum(weights, axis=-1, keepdims=True)
        kept.append(weights.astype(BF16))
        put(rows + row, jnp.where(lane < width // 2, top, total))
    for copy in v_copies:
        copy.wait()
    for row in range(rows):
        summed = jnp.zeros((heads, width), F32)
        for at in range(0, pages, PAGES_PER_DOT):
            summed += jnp.dot(
                kept[row][:, at * cells : (at + PAGES_PER_DOT) * cells],
                block(v_vmem, row, at),
                preferred_element_type=F32,
            )
        put(row, summed)


def pack(out, means, log_total):
    heads = len(means)
    copies = out.shape[0]
    for h in range(heads):
        mean = means[h].astype(BF16)
        for i in range(copies):
            out[i, h] = mean
    first = log_total.astype(BF16).astype(F32)
    second = (log_total - first).astype(BF16).astype(F32)
    third = log_total - first - second
    rest = jnp.zeros((first.shape[0], out.shape[-1] - 3 * heads), F32)
    terms = jnp.concatenate([first, second, third, rest], axis=1).astype(BF16)
    for i in range(copies):
        out[i, heads] = terms


def merge_cores_kernel(keep, received, out):
    heads, double, width = keep.shape
    rows = double // 2
    mine, theirs = keep[...], received[...]

    def stats(block):
        return block[:, rows:, 0:1], block[:, rows:, width // 2 : width // 2 + 1]

    top_a, total_a = stats(mine)
    top_b, total_b = stats(theirs)
    top = jnp.maximum(top_a, top_b)
    factor_a, factor_b = jnp.exp(top_a - top), jnp.exp(top_b - top)
    total = factor_a * total_a + factor_b * total_b
    summed = factor_a * mine[:, :rows, :] + factor_b * theirs[:, :rows, :]
    live = total > 0.0
    safe = jnp.where(live, total, 1.0)
    mean = jnp.where(live, summed / safe, 0.0)
    log_total = jnp.where(live, top + jnp.log(safe), NEG)
    shape = (heads, rows, width)
    here = lax.broadcasted_iota(jnp.int32, shape, 2) == lax.broadcasted_iota(jnp.int32, shape, 0)
    pack(out, list(mean), jnp.sum(jnp.where(here, log_total, 0.0), axis=0)[:, :heads])


def merge_chips_kernel(parts, out):
    count = parts.shape[0]
    heads = parts.shape[1] - 1
    logs = []
    for i in range(count):
        terms = parts[i, heads].astype(F32)
        logs.append(terms[:, :heads] + terms[:, heads : 2 * heads] + terms[:, 2 * heads : 3 * heads])
    top = functools.reduce(jnp.maximum, logs)
    factors = [jnp.exp(log - top) for log in logs]
    total = functools.reduce(jnp.add, factors)
    shares = [factor / total for factor in factors]
    for h in range(heads):
        out[h] = functools.reduce(
            jnp.add, [shares[i][:, h : h + 1] * parts[i, h].astype(F32) for i in range(count)]
        ).astype(BF16)


def join_kernel(*refs):
    for i in range(refs[-1].shape[0]):
        refs[-1][i] = refs[i][...]


def feed_kernel(
    mine,
    theirs,
    residual,
    gain,
    gate_w,
    up_h,
    down_h,
    out,
    share_out,
    up_w,
    down_w,
    hidden,
    normed,
    sems,
):
    groups, half, rows, width = mine.shape
    count = groups * half * 2
    features = count * width
    kv, tp = kv_index(), lax.axis_index("tp")
    in_step = features // IN_STEPS
    out_step = features // OUT_STEPS

    def pieces(source, target, which, steps):
        step = features // steps
        copies = []
        for i in range(steps):
            at = pl.ds(i * step, step)
            copies.append(
                pltpu.make_async_copy(source.at[:, at], target.at[:, at], sems.at[which, i])
            )
        return copies

    up_copies = pieces(up_h, up_w, 0, IN_STEPS)
    down_copies = pieces(down_h, down_w, 1, OUT_STEPS)
    for copy in up_copies + down_copies:
        copy.start()
    squares = jnp.zeros((rows, width), F32)
    for part, core in ((mine, kv % 2), (theirs, 1 - kv % 2)):
        for distance in range(groups):
            base = ((tp + distance) % groups) * (2 * half) + core * half
            for i in range(half):
                cols = pl.ds(pl.multiple_of((base + i) * width, width), width)
                value = residual[:, cols].astype(F32) + part[distance, i].astype(F32)
                hidden[base + i] = value
                squares += value * value
    mean_square = jnp.sum(squares, axis=-1, keepdims=True) / features
    scale = lax.rsqrt(mean_square + 1e-05)
    for i in range(count):
        cols = slice(i * width, (i + 1) * width)
        normed[:, cols] = (hidden[i] * scale * gain[i : i + 1, :].astype(F32)).astype(BF16)
    share_out[...] = hidden[kv * groups + tp]
    units = gate_w.shape[0]
    gate = jnp.zeros((rows, units), F32)
    up = jnp.zeros((rows, units), F32)
    for i in range(IN_STEPS):
        at = i * in_step
        x = normed[:, at : at + in_step]
        up_copies[i].wait()
        gate += lax.dot_general(x, gate_w[:, at : at + in_step], NT, preferred_element_type=F32)
        up += lax.dot_general(x, up_w[:, at : at + in_step], NT, preferred_element_type=F32)
    activated = (gate / (1.0 + jnp.exp(-gate)) * up).astype(BF16)
    for i in range(OUT_STEPS):
        at = i * out_step
        down_copies[i].wait()
        for half in range(at, at + out_step, CHUNK):
            mixed = jnp.dot(activated, down_w[:, half : half + CHUNK], preferred_element_type=F32)
            for j in range(CHUNK // width):
                out[half // width + j] = mixed[:, j * width : (j + 1) * width]


def load_kernel(after, *refs):
    count = len(refs) // 2
    sems = refs[2 * count]
    copies = []
    for i in range(count):
        copies.append(pltpu.make_async_copy(refs[i], refs[count + i], sems.at[i]))
    for copy in copies:
        copy.start()
    for copy in copies:
        copy.wait()


def load(after, *arrays):
    moved = sum(2 * x.size for x in arrays)
    return pl.pallas_call(
        load_kernel,
        out_shape=[pltpu.VMEM(x.shape, BF16) for x in arrays],
        in_specs=[VMEM] + [HBM] * len(arrays),
        out_specs=[VMEM] * len(arrays),
        scratch_shapes=[pltpu.SemaphoreType.DMA((len(arrays),))],
        compiler_params=pltpu.CompilerParams(vmem_limit_bytes=16 * MIB),
        cost_estimate=pl.CostEstimate(flops=0, bytes_accessed=moved, transcendentals=0),
        name="load_weights",
    )(after, *in_hbm(*arrays))


def own_heads_kernel(finished, theirs, share, out):
    half, rows, width = finished.shape
    first = lax.axis_index("core") == 0
    mine, other = finished[...].astype(F32), theirs[0].astype(F32)
    low = jnp.where(first, mine, other)
    high = jnp.where(first, other, mine)
    for row in range(rows):
        out[row, :half] = low[:, row, :].astype(BF16)
        out[row, half:] = high[:, row, :].astype(BF16)


def final_kernel(parts, share, out):
    out[...] = (share[...] + jnp.sum(parts[...], axis=0)).astype(BF16)


VMEM = pl.BlockSpec(memory_space=pltpu.VMEM)
HBM = pl.BlockSpec(memory_space=pltpu.HBM)


def in_hbm(*arrays):
    return [pltpu.with_memory_space_constraint(x, pltpu.HBM) for x in arrays]


def shards(
    query,
    key_cache,
    value_cache,
    seq_lengths,
    block_table,
    residual,
    norm_gain,
    gate_weight,
    up_weight,
    down_weight,
):
    rows, heads, width = query.shape
    keys = key_cache.reshape(-1, width)
    values = value_cache.reshape(-1, width)
    kv_size, tp_size = lax.axis_size("chip") * lax.axis_size("core"), lax.axis_size("tp")
    devices = kv_size * tp_size
    half = heads // 2
    small = pltpu.CompilerParams(vmem_limit_bytes=16 * MIB)
    block_f32 = jax.ShapeDtypeStruct((half, 2 * rows, width), F32)
    packed = jax.ShapeDtypeStruct((lax.axis_size("chip"), half + 1, rows, width), BF16)
    keep, send = pl.pallas_call(
        attention_kernel,
        out_shape=[block_f32] * 2,
        in_specs=[HBM] * 5,
        out_specs=[VMEM] * 2,
        scratch_shapes=[
            pltpu.SMEM(seq_lengths.shape, jnp.int32),
            pltpu.SMEM(block_table.shape, jnp.int32),
            pltpu.VMEM(query.shape, BF16),
            pltpu.VMEM(keys.shape, BF16),
            pltpu.VMEM(values.shape, BF16),
            pltpu.SemaphoreType.DMA((3 + 2 * PARTS,)),
        ],
        compiler_params=small,
        name="attention_partials",
    )(*in_hbm(seq_lengths, block_table, query, keys, values))

    def call(kernel, out_shape, name, *operands):
        return pl.pallas_call(
            kernel,
            out_shape=out_shape,
            in_specs=[VMEM] * len(operands),
            out_specs=VMEM,
            compiler_params=small,
            name=name,
        )(*operands)

    def ring(x):
        one, three, two = (
            lax.ppermute(x, "tp", [(i, (i - distance) % tp_size) for i in range(tp_size)])
            for distance in (1, 3, 2)
        )
        return one, two, three

    swap = [(0, 1), (1, 0)]
    block = call(
        merge_cores_kernel, packed, "merge_cores", keep, lax.ppermute(send, "core", swap)
    )
    blocks = lax.all_to_all(block, "chip", 0, 0, tiled=True)
    finished = call(
        merge_chips_kernel,
        jax.ShapeDtypeStruct((half, rows, width), BF16),
        "merge_chips",
        blocks,
    )
    around = ring(finished)
    gate, res, gain = load(
        finished, gate_weight, residual, norm_gain.reshape(devices, width)
    )
    mine = call(
        join_kernel,
        jax.ShapeDtypeStruct((tp_size, half, rows, width), BF16),
        "join_heads",
        finished,
        *around,
        gain,
    )
    theirs = lax.ppermute(mine, "core", swap)
    mixed, share = pl.pallas_call(
        feed_kernel,
        out_shape=[
            jax.ShapeDtypeStruct((devices, rows, width), F32),
            jax.ShapeDtypeStruct((rows, width), F32),
        ],
        in_specs=[VMEM] * 5 + [HBM] * 2,
        out_specs=[VMEM] * 2,
        scratch_shapes=[
            pltpu.VMEM(up_weight.shape, BF16),
            pltpu.VMEM(down_weight.shape, BF16),
            pltpu.VMEM((devices, rows, width), F32),
            pltpu.VMEM((rows, devices * width), BF16),
            pltpu.SemaphoreType.DMA((2, IN_STEPS)),
        ],
        compiler_params=pltpu.CompilerParams(vmem_limit_bytes=32 * MIB),
        name="feed_forward",
    )(
        mine,
        theirs,
        res,
        gain,
        gate,
        *in_hbm(up_weight, down_weight),
    )
    sums = lax.all_to_all(mixed, ("chip", "core", "tp"), 0, 0, tiled=True)
    layer_out = call(
        final_kernel, jax.ShapeDtypeStruct((rows, width), BF16), "add_shares", sums, share
    )
    attention = call(
        own_heads_kernel,
        jax.ShapeDtypeStruct(query.shape, BF16),
        "own_heads",
        finished,
        theirs,
        share,
    )
    return layer_out, attention


def solution(mesh):
    devices = mesh.devices
    split = Mesh(devices.reshape(-1, 2, devices.shape[1]), ("chip", "core", "tp"))
    kv = ("chip", "core")
    every = ("chip", "core", "tp")
    placed = (
        P(None, "tp", None),
        P(kv, None, "tp", None),
        P(kv, None, "tp", None),
        P(),
        P(None, kv),
        P(),
        P(),
        P(every, None),
        P(every, None),
        P(every, None),
    )
    return jax.shard_map(
        shards,
        mesh=split,
        in_specs=placed,
        out_specs=(P(None, every), P(None, "tp", None)),
        check_vma=False,
    )
```

```python
import functools

import jax
import jax.numpy as jnp
from jax import lax
from jax.experimental import pallas as pl
from jax.experimental.pallas import tpu as pltpu
from jax.sharding import Mesh
from jax.sharding import PartitionSpec as P

NEG = -1e30
F32 = jnp.float32
BF16 = jnp.bfloat16
MIB = 1 << 20
NT = (((1,), (1,)), ((), ()))
PAGES_PER_DOT = 8
PARTS = 4
CHUNK = 2048
IN_STEPS = 8
OUT_STEPS = 4


def kv_index():
    return lax.axis_index("chip") * lax.axis_size("core") + lax.axis_index("core")


def attention_kernel(
    lengths_h, table_h, query_h, keys, values, keep, send, lengths, table, query, k_vmem, v_vmem, sems
):
    rows, heads, width = query.shape
    pages = table.shape[1]
    cells = keys.shape[0] // (rows * pages)
    small = [
        pltpu.make_async_copy(table_h, table, sems.at[0]),
        pltpu.make_async_copy(lengths_h, lengths, sems.at[1]),
        pltpu.make_async_copy(query_h, query, sems.at[2]),
    ]
    part = keys.shape[0] // PARTS
    k_copies, v_copies = [], []
    for i in range(PARTS):
        at = pl.ds(i * part, part)
        k_copies.append(pltpu.make_async_copy(keys.at[at], k_vmem.at[at], sems.at[3 + i]))
        v_copies.append(pltpu.make_async_copy(values.at[at], v_vmem.at[at], sems.at[3 + PARTS + i]))
    for copy in small + k_copies + v_copies:
        copy.start()
    first = kv_index() * (pages * cells // 2)
    span = pages * cells
    column = lax.broadcasted_iota(jnp.int32, (heads, span), 1)
    head = lax.broadcasted_iota(jnp.int32, (heads, span), 0)
    own = (column % 2) == (head // (heads // 2))
    position = jnp.where(own, first + column // 2, jnp.int32(2**30))
    lane = lax.broadcasted_iota(jnp.int32, (heads, width), 1)
    half = heads // 2
    core = lax.axis_index("core")

    def put(row, block):
        low, high = block[:half], block[half:]
        keep[:, row, :] = jnp.where(core == 0, low, high)
        send[:, row, :] = jnp.where(core == 0, high, low)

    def block(ref, row, at):
        return jnp.concatenate(
            [
                ref[pl.ds(pl.multiple_of(table[row, at + i] * cells, cells), cells), :]
                for i in range(PAGES_PER_DOT)
            ],
            axis=0,
        )

    kept = []
    for copy in small + k_copies:
        copy.wait()
    for row in range(rows):
        q = query[row]
        scores = jnp.concatenate(
            [
                lax.dot_general(q, block(k_vmem, row, at), NT, preferred_element_type=F32)
                for at in range(0, pages, PAGES_PER_DOT)
            ],
            axis=1,
        ) * (width**-0.5)
        active = position < lengths[row]
        masked = jnp.where(active, scores, NEG)
        top = jnp.max(masked, axis=-1, keepdims=True)
        weights = jnp.where(active, jnp.exp(masked - top), 0.0)
        total = jnp.sum(weights, axis=-1, keepdims=True)
        kept.append(weights.astype(BF16))
        put(rows + row, jnp.where(lane < width // 2, top, total))
    for copy in v_copies:
        copy.wait()
    for row in range(rows):
        summed = jnp.zeros((heads, width), F32)
        for at in range(0, pages, PAGES_PER_DOT):
            summed += jnp.dot(
                kept[row][:, at * cells : (at + PAGES_PER_DOT) * cells],
                block(v_vmem, row, at),
                preferred_element_type=F32,
            )
        put(row, summed)


def pack(out, means, log_total):
    heads = len(means)
    copies = out.shape[0]
    for h in range(heads):
        mean = means[h].astype(BF16)
        for i in range(copies):
            out[i, h] = mean
    first = log_total.astype(BF16).astype(F32)
    second = (log_total - first).astype(BF16).astype(F32)
    third = log_total - first - second
    rest = jnp.zeros((first.shape[0], out.shape[-1] - 3 * heads), F32)
    terms = jnp.concatenate([first, second, third, rest], axis=1).astype(BF16)
    for i in range(copies):
        out[i, heads] = terms


def merge_cores_kernel(keep, received, out):
    heads, double, width = keep.shape
    rows = double // 2
    mine, theirs = keep[...], received[...]

    def stats(block):
        return block[:, rows:, 0:1], block[:, rows:, width // 2 : width // 2 + 1]

    top_a, total_a = stats(mine)
    top_b, total_b = stats(theirs)
    top = jnp.maximum(top_a, top_b)
    factor_a, factor_b = jnp.exp(top_a - top), jnp.exp(top_b - top)
    total = factor_a * total_a + factor_b * total_b
    summed = factor_a * mine[:, :rows, :] + factor_b * theirs[:, :rows, :]
    live = total > 0.0
    safe = jnp.where(live, total, 1.0)
    mean = jnp.where(live, summed / safe, 0.0)
    log_total = jnp.where(live, top + jnp.log(safe), NEG)
    shape = (heads, rows, width)
    here = lax.broadcasted_iota(jnp.int32, shape, 2) == lax.broadcasted_iota(jnp.int32, shape, 0)
    pack(out, list(mean), jnp.sum(jnp.where(here, log_total, 0.0), axis=0)[:, :heads])


def merge_chips_kernel(parts, out):
    count = parts.shape[0]
    heads = parts.shape[1] - 1
    logs = []
    for i in range(count):
        terms = parts[i, heads].astype(F32)
        logs.append(terms[:, :heads] + terms[:, heads : 2 * heads] + terms[:, 2 * heads : 3 * heads])
    top = functools.reduce(jnp.maximum, logs)
    factors = [jnp.exp(log - top) for log in logs]
    total = functools.reduce(jnp.add, factors)
    shares = [factor / total for factor in factors]
    for h in range(heads):
        out[h] = functools.reduce(
            jnp.add, [shares[i][:, h : h + 1] * parts[i, h].astype(F32) for i in range(count)]
        ).astype(BF16)


def join_kernel(*refs):
    for i in range(refs[-1].shape[0]):
        refs[-1][i] = refs[i][...]


def feed_kernel(
    mine,
    theirs,
    residual,
    gain,
    gate_w,
    up_h,
    down_h,
    out,
    share_out,
    up_w,
    down_w,
    hidden,
    normed,
    sems,
):
    groups, half, rows, width = mine.shape
    count = groups * half * 2
    features = count * width
    kv, tp = kv_index(), lax.axis_index("tp")
    in_step = features // IN_STEPS
    out_step = features // OUT_STEPS

    def pieces(source, target, which, steps):
        step = features // steps
        copies = []
        for i in range(steps):
            at = pl.ds(i * step, step)
            copies.append(
                pltpu.make_async_copy(source.at[:, at], target.at[:, at], sems.at[which, i])
            )
        return copies

    up_copies = pieces(up_h, up_w, 0, IN_STEPS)
    down_copies = pieces(down_h, down_w, 1, OUT_STEPS)
    for copy in up_copies + down_copies:
        copy.start()
    squares = jnp.zeros((rows, width), F32)
    for part, core in ((mine, kv % 2), (theirs, 1 - kv % 2)):
        for distance in range(groups):
            base = ((tp + distance) % groups) * (2 * half) + core * half
            for i in range(half):
                cols = pl.ds(pl.multiple_of((base + i) * width, width), width)
                value = residual[:, cols].astype(F32) + part[distance, i].astype(F32)
                hidden[base + i] = value
                squares += value * value
    mean_square = jnp.sum(squares, axis=-1, keepdims=True) / features
    scale = lax.rsqrt(mean_square + 1e-05)
    for i in range(count):
        cols = slice(i * width, (i + 1) * width)
        normed[:, cols] = (hidden[i] * scale * gain[i : i + 1, :].astype(F32)).astype(BF16)
    share_out[...] = hidden[kv * groups + tp]
    units = gate_w.shape[0]
    gate = jnp.zeros((rows, units), F32)
    up = jnp.zeros((rows, units), F32)
    for i in range(IN_STEPS):
        at = i * in_step
        x = normed[:, at : at + in_step]
        up_copies[i].wait()
        gate += lax.dot_general(x, gate_w[:, at : at + in_step], NT, preferred_element_type=F32)
        up += lax.dot_general(x, up_w[:, at : at + in_step], NT, preferred_element_type=F32)
    activated = (gate / (1.0 + jnp.exp(-gate)) * up).astype(BF16)
    for i in range(OUT_STEPS):
        at = i * out_step
        down_copies[i].wait()
        for half in range(at, at + out_step, CHUNK):
            mixed = jnp.dot(activated, down_w[:, half : half + CHUNK], preferred_element_type=F32)
            for j in range(CHUNK // width):
                out[half // width + j] = mixed[:, j * width : (j + 1) * width].astype(BF16)


def load_kernel(after, *refs):
    count = len(refs) // 2
    sems = refs[2 * count]
    copies = []
    for i in range(count):
        copies.append(pltpu.make_async_copy(refs[i], refs[count + i], sems.at[i]))
    for copy in copies:
        copy.start()
    for copy in copies:
        copy.wait()


def load(after, *arrays):
    moved = sum(2 * x.size for x in arrays)
    return pl.pallas_call(
        load_kernel,
        out_shape=[pltpu.VMEM(x.shape, BF16) for x in arrays],
        in_specs=[VMEM] + [HBM] * len(arrays),
        out_specs=[VMEM] * len(arrays),
        scratch_shapes=[pltpu.SemaphoreType.DMA((len(arrays),))],
        compiler_params=pltpu.CompilerParams(vmem_limit_bytes=16 * MIB),
        cost_estimate=pl.CostEstimate(flops=0, bytes_accessed=moved, transcendentals=0),
        name="load_weights",
    )(after, *in_hbm(*arrays))


def own_heads_kernel(finished, theirs, share, out):
    half, rows, width = finished.shape
    first = lax.axis_index("core") == 0
    mine, other = finished[...].astype(F32), theirs[0].astype(F32)
    low = jnp.where(first, mine, other)
    high = jnp.where(first, other, mine)
    for row in range(rows):
        out[row, :half] = low[:, row, :].astype(BF16)
        out[row, half:] = high[:, row, :].astype(BF16)


def final_kernel(parts, share, out):
    terms = [parts[i].astype(F32) for i in range(parts.shape[0])]
    while len(terms) > 1:
        terms = [terms[i] + terms[i + 1] for i in range(0, len(terms), 2)]
    out[...] = (share[...] + terms[0]).astype(BF16)


VMEM = pl.BlockSpec(memory_space=pltpu.VMEM)
HBM = pl.BlockSpec(memory_space=pltpu.HBM)


def in_hbm(*arrays):
    return [pltpu.with_memory_space_constraint(x, pltpu.HBM) for x in arrays]


def shards(
    query,
    key_cache,
    value_cache,
    seq_lengths,
    block_table,
    residual,
    norm_gain,
    gate_weight,
    up_weight,
    down_weight,
):
    rows, heads, width = query.shape
    keys = key_cache.reshape(-1, width)
    values = value_cache.reshape(-1, width)
    kv_size, tp_size = lax.axis_size("chip") * lax.axis_size("core"), lax.axis_size("tp")
    devices = kv_size * tp_size
    half = heads // 2
    small = pltpu.CompilerParams(vmem_limit_bytes=16 * MIB)
    block_f32 = jax.ShapeDtypeStruct((half, 2 * rows, width), F32)
    packed = jax.ShapeDtypeStruct((lax.axis_size("chip"), half + 1, rows, width), BF16)
    keep, send = pl.pallas_call(
        attention_kernel,
        out_shape=[block_f32] * 2,
        in_specs=[HBM] * 5,
        out_specs=[VMEM] * 2,
        scratch_shapes=[
            pltpu.SMEM(seq_lengths.shape, jnp.int32),
            pltpu.SMEM(block_table.shape, jnp.int32),
            pltpu.VMEM(query.shape, BF16),
            pltpu.VMEM(keys.shape, BF16),
            pltpu.VMEM(values.shape, BF16),
            pltpu.SemaphoreType.DMA((3 + 2 * PARTS,)),
        ],
        compiler_params=small,
        name="attention_partials",
    )(*in_hbm(seq_lengths, block_table, query, keys, values))

    def call(kernel, out_shape, name, *operands):
        return pl.pallas_call(
            kernel,
            out_shape=out_shape,
            in_specs=[VMEM] * len(operands),
            out_specs=VMEM,
            compiler_params=small,
            name=name,
        )(*operands)

    def ring(x):
        one, three, two = (
            lax.ppermute(x, "tp", [(i, (i - distance) % tp_size) for i in range(tp_size)])
            for distance in (1, 3, 2)
        )
        return one, two, three

    swap = [(0, 1), (1, 0)]
    block = call(
        merge_cores_kernel, packed, "merge_cores", keep, lax.ppermute(send, "core", swap)
    )
    blocks = lax.all_to_all(block, "chip", 0, 0, tiled=True)
    finished = call(
        merge_chips_kernel,
        jax.ShapeDtypeStruct((half, rows, width), BF16),
        "merge_chips",
        blocks,
    )
    around = ring(finished)
    gate, res, gain = load(
        finished, gate_weight, residual, norm_gain.reshape(devices, width)
    )
    mine = call(
        join_kernel,
        jax.ShapeDtypeStruct((tp_size, half, rows, width), BF16),
        "join_heads",
        finished,
        *around,
        gain,
    )
    theirs = lax.ppermute(mine, "core", swap)
    mixed, share = pl.pallas_call(
        feed_kernel,
        out_shape=[
            jax.ShapeDtypeStruct((devices, rows, width), BF16),
            jax.ShapeDtypeStruct((rows, width), F32),
        ],
        in_specs=[VMEM] * 5 + [HBM] * 2,
        out_specs=[VMEM] * 2,
        scratch_shapes=[
            pltpu.VMEM(up_weight.shape, BF16),
            pltpu.VMEM(down_weight.shape, BF16),
            pltpu.VMEM((devices, rows, width), F32),
            pltpu.VMEM((rows, devices * width), BF16),
            pltpu.SemaphoreType.DMA((2, IN_STEPS)),
        ],
        compiler_params=pltpu.CompilerParams(vmem_limit_bytes=32 * MIB),
        name="feed_forward",
    )(
        mine,
        theirs,
        res,
        gain,
        gate,
        *in_hbm(up_weight, down_weight),
    )
    sums = lax.all_to_all(mixed, ("chip", "core", "tp"), 0, 0, tiled=True)
    layer_out = call(
        final_kernel, jax.ShapeDtypeStruct((rows, width), BF16), "add_shares", sums, share
    )
    attention = call(
        own_heads_kernel,
        jax.ShapeDtypeStruct(query.shape, BF16),
        "own_heads",
        finished,
        theirs,
        share,
    )
    return layer_out, attention


def solution(mesh):
    devices = mesh.devices
    split = Mesh(devices.reshape(-1, 2, devices.shape[1]), ("chip", "core", "tp"))
    kv = ("chip", "core")
    every = ("chip", "core", "tp")
    placed = (
        P(None, "tp", None),
        P(kv, None, "tp", None),
        P(kv, None, "tp", None),
        P(),
        P(None, kv),
        P(),
        P(),
        P(every, None),
        P(every, None),
        P(every, None),
    )
    return jax.shard_map(
        shards,
        mesh=split,
        in_specs=placed,
        out_specs=(P(None, every), P(None, "tp", None)),
        check_vma=False,
    )
```

```python
import functools

import jax
import jax.numpy as jnp
from jax import lax
from jax.experimental import pallas as pl
from jax.experimental.pallas import tpu as pltpu
from jax.sharding import Mesh
from jax.sharding import PartitionSpec as P

NEG = -1e30
F32 = jnp.float32
BF16 = jnp.bfloat16
MIB = 1 << 20
NT = (((1,), (1,)), ((), ()))
PAGES_PER_DOT = 8
PARTS = 8
CHUNK = 2048
IN_STEPS = 8
OUT_STEPS = 4


def kv_index():
    return lax.axis_index("chip") * lax.axis_size("core") + lax.axis_index("core")


def attention_kernel(
    lengths_h, table_h, query_h, keys, values, keep, send, lengths, table, query, k_vmem, v_vmem, sems
):
    rows, heads, width = query.shape
    pages = table.shape[1]
    cells = keys.shape[0] // (rows * pages)
    small = [
        pltpu.make_async_copy(table_h, table, sems.at[0]),
        pltpu.make_async_copy(lengths_h, lengths, sems.at[1]),
        pltpu.make_async_copy(query_h, query, sems.at[2]),
    ]
    part = keys.shape[0] // PARTS
    k_copies, v_copies = [], []
    for i in range(PARTS):
        at = pl.ds(i * part, part)
        k_copies.append(pltpu.make_async_copy(keys.at[at], k_vmem.at[at], sems.at[3 + i]))
        v_copies.append(pltpu.make_async_copy(values.at[at], v_vmem.at[at], sems.at[3 + PARTS + i]))
    for copy in small + k_copies + v_copies:
        copy.start()
    first = kv_index() * (pages * cells // 2)
    span = pages * cells
    column = lax.broadcasted_iota(jnp.int32, (heads, span), 1)
    head = lax.broadcasted_iota(jnp.int32, (heads, span), 0)
    own = (column % 2) == (head // (heads // 2))
    position = jnp.where(own, first + column // 2, jnp.int32(2**30))
    lane = lax.broadcasted_iota(jnp.int32, (heads, width), 1)
    half = heads // 2
    core = lax.axis_index("core")

    def put(row, block):
        low, high = block[:half], block[half:]
        keep[:, row, :] = jnp.where(core == 0, low, high)
        send[:, row, :] = jnp.where(core == 0, high, low)

    def block(ref, row, at):
        return jnp.concatenate(
            [
                ref[pl.ds(pl.multiple_of(table[row, at + i] * cells, cells), cells), :]
                for i in range(PAGES_PER_DOT)
            ],
            axis=0,
        )

    kept = []
    for copy in small + k_copies:
        copy.wait()
    for row in range(rows):
        q = query[row]
        scores = jnp.concatenate(
            [
                lax.dot_general(q, block(k_vmem, row, at), NT, preferred_element_type=F32)
                for at in range(0, pages, PAGES_PER_DOT)
            ],
            axis=1,
        ) * (width**-0.5)
        active = position < lengths[row]
        masked = jnp.where(active, scores, NEG)
        top = jnp.max(masked, axis=-1, keepdims=True)
        weights = jnp.where(active, jnp.exp(masked - top), 0.0)
        total = jnp.sum(weights, axis=-1, keepdims=True)
        kept.append(weights.astype(BF16))
        put(rows + row, jnp.where(lane < width // 2, top, total))
    for copy in v_copies:
        copy.wait()
    for row in range(rows):
        summed = jnp.zeros((heads, width), F32)
        for at in range(0, pages, PAGES_PER_DOT):
            summed += jnp.dot(
                kept[row][:, at * cells : (at + PAGES_PER_DOT) * cells],
                block(v_vmem, row, at),
                preferred_element_type=F32,
            )
        put(row, summed)


def pack(out, means, log_total):
    heads = len(means)
    copies = out.shape[0]
    for h in range(heads):
        mean = means[h].astype(BF16)
        for i in range(copies):
            out[i, h] = mean
    first = log_total.astype(BF16).astype(F32)
    second = (log_total - first).astype(BF16).astype(F32)
    third = log_total - first - second
    rest = jnp.zeros((first.shape[0], out.shape[-1] - 3 * heads), F32)
    terms = jnp.concatenate([first, second, third, rest], axis=1).astype(BF16)
    for i in range(copies):
        out[i, heads] = terms


def merge_cores_kernel(keep, received, out):
    heads, double, width = keep.shape
    rows = double // 2
    mine, theirs = keep[...], received[...]

    def stats(block):
        return block[:, rows:, 0:1], block[:, rows:, width // 2 : width // 2 + 1]

    top_a, total_a = stats(mine)
    top_b, total_b = stats(theirs)
    top = jnp.maximum(top_a, top_b)
    factor_a, factor_b = jnp.exp(top_a - top), jnp.exp(top_b - top)
    total = factor_a * total_a + factor_b * total_b
    summed = factor_a * mine[:, :rows, :] + factor_b * theirs[:, :rows, :]
    live = total > 0.0
    safe = jnp.where(live, total, 1.0)
    mean = jnp.where(live, summed / safe, 0.0)
    log_total = jnp.where(live, top + jnp.log(safe), NEG)
    shape = (heads, rows, width)
    here = lax.broadcasted_iota(jnp.int32, shape, 2) == lax.broadcasted_iota(jnp.int32, shape, 0)
    pack(out, list(mean), jnp.sum(jnp.where(here, log_total, 0.0), axis=0)[:, :heads])


def merge_chips_kernel(parts, out):
    count = parts.shape[0]
    heads = parts.shape[1] - 1
    logs = []
    for i in range(count):
        terms = parts[i, heads].astype(F32)
        logs.append(terms[:, :heads] + terms[:, heads : 2 * heads] + terms[:, 2 * heads : 3 * heads])
    top = functools.reduce(jnp.maximum, logs)
    factors = [jnp.exp(log - top) for log in logs]
    total = functools.reduce(jnp.add, factors)
    shares = [factor / total for factor in factors]
    for h in range(heads):
        out[h] = functools.reduce(
            jnp.add, [shares[i][:, h : h + 1] * parts[i, h].astype(F32) for i in range(count)]
        ).astype(BF16)


def join_kernel(*refs):
    for i in range(refs[-1].shape[0]):
        refs[-1][i] = refs[i][...]


def feed_kernel(
    mine,
    theirs,
    residual,
    gain,
    gate_w,
    up_h,
    down_h,
    out,
    share_out,
    up_w,
    down_w,
    hidden,
    normed,
    sems,
):
    groups, half, rows, width = mine.shape
    count = groups * half * 2
    features = count * width
    kv, tp = kv_index(), lax.axis_index("tp")
    in_step = features // IN_STEPS
    out_step = features // OUT_STEPS

    def pieces(source, target, which, steps):
        step = features // steps
        copies = []
        for i in range(steps):
            at = pl.ds(i * step, step)
            copies.append(
                pltpu.make_async_copy(source.at[:, at], target.at[:, at], sems.at[which, i])
            )
        return copies

    up_copies = pieces(up_h, up_w, 0, IN_STEPS)
    down_copies = pieces(down_h, down_w, 1, OUT_STEPS)
    for copy in up_copies + down_copies:
        copy.start()
    squares = jnp.zeros((rows, width), F32)
    for part, core in ((mine, kv % 2), (theirs, 1 - kv % 2)):
        for distance in range(groups):
            held = core if distance == 0 else 1 - core
            base = ((tp + distance) % groups) * (2 * half) + held * half
            for i in range(half):
                cols = pl.ds(pl.multiple_of((base + i) * width, width), width)
                value = residual[:, cols].astype(F32) + part[distance, i].astype(F32)
                hidden[base + i] = value
                squares += value * value
    mean_square = jnp.sum(squares, axis=-1, keepdims=True) / features
    scale = lax.rsqrt(mean_square + 1e-05)
    for i in range(count):
        cols = slice(i * width, (i + 1) * width)
        normed[:, cols] = (hidden[i] * scale * gain[i : i + 1, :].astype(F32)).astype(BF16)
    share_out[...] = hidden[kv * groups + tp]
    units = gate_w.shape[0]
    gate = jnp.zeros((rows, units), F32)
    up = jnp.zeros((rows, units), F32)
    for i in range(IN_STEPS):
        at = i * in_step
        x = normed[:, at : at + in_step]
        up_copies[i].wait()
        gate += lax.dot_general(x, gate_w[:, at : at + in_step], NT, preferred_element_type=F32)
        up += lax.dot_general(x, up_w[:, at : at + in_step], NT, preferred_element_type=F32)
    activated = (gate / (1.0 + jnp.exp(-gate)) * up).astype(BF16)
    for i in range(OUT_STEPS):
        at = i * out_step
        down_copies[i].wait()
        for half in range(at, at + out_step, CHUNK):
            mixed = jnp.dot(activated, down_w[:, half : half + CHUNK], preferred_element_type=F32)
            for j in range(CHUNK // width):
                out[half // width + j] = mixed[:, j * width : (j + 1) * width].astype(BF16)


def load_kernel(after, *refs):
    count = len(refs) // 2
    sems = refs[2 * count]
    copies = []
    for i in range(count):
        copies.append(pltpu.make_async_copy(refs[i], refs[count + i], sems.at[i]))
    for copy in copies:
        copy.start()
    for copy in copies:
        copy.wait()


def load(after, *arrays):
    moved = sum(2 * x.size for x in arrays)
    return pl.pallas_call(
        load_kernel,
        out_shape=[pltpu.VMEM(x.shape, BF16) for x in arrays],
        in_specs=[VMEM] + [HBM] * len(arrays),
        out_specs=[VMEM] * len(arrays),
        scratch_shapes=[pltpu.SemaphoreType.DMA((len(arrays),))],
        compiler_params=pltpu.CompilerParams(vmem_limit_bytes=16 * MIB),
        cost_estimate=pl.CostEstimate(flops=0, bytes_accessed=moved, transcendentals=0),
        name="load_weights",
    )(after, *in_hbm(*arrays))


def final_kernel(parts, share, finished, theirs, layer_out, attention):
    half, rows, width = finished.shape
    first = lax.axis_index("core") == 0
    mine, other = finished[...].astype(F32), theirs[0].astype(F32)
    low = jnp.where(first, mine, other)
    high = jnp.where(first, other, mine)
    for row in range(rows):
        attention[row, :half] = low[:, row, :].astype(BF16)
        attention[row, half:] = high[:, row, :].astype(BF16)
    terms = [parts[i].astype(F32) for i in range(parts.shape[0])]
    while len(terms) > 1:
        terms = [terms[i] + terms[i + 1] for i in range(0, len(terms), 2)]
    layer_out[...] = (share[...] + terms[0]).astype(BF16)


VMEM = pl.BlockSpec(memory_space=pltpu.VMEM)
HBM = pl.BlockSpec(memory_space=pltpu.HBM)


def in_hbm(*arrays):
    return [pltpu.with_memory_space_constraint(x, pltpu.HBM) for x in arrays]


def shards(
    query,
    key_cache,
    value_cache,
    seq_lengths,
    block_table,
    residual,
    norm_gain,
    gate_weight,
    up_weight,
    down_weight,
):
    rows, heads, width = query.shape
    keys = key_cache.reshape(-1, width)
    values = value_cache.reshape(-1, width)
    kv_size, tp_size = lax.axis_size("chip") * lax.axis_size("core"), lax.axis_size("tp")
    devices = kv_size * tp_size
    half = heads // 2
    small = pltpu.CompilerParams(vmem_limit_bytes=16 * MIB)
    block_f32 = jax.ShapeDtypeStruct((half, 2 * rows, width), F32)
    packed = jax.ShapeDtypeStruct((lax.axis_size("chip"), half + 1, rows, width), BF16)
    keep, send = pl.pallas_call(
        attention_kernel,
        out_shape=[block_f32] * 2,
        in_specs=[HBM] * 5,
        out_specs=[VMEM] * 2,
        scratch_shapes=[
            pltpu.SMEM(seq_lengths.shape, jnp.int32),
            pltpu.SMEM(block_table.shape, jnp.int32),
            pltpu.VMEM(query.shape, BF16),
            pltpu.VMEM(keys.shape, BF16),
            pltpu.VMEM(values.shape, BF16),
            pltpu.SemaphoreType.DMA((3 + 2 * PARTS,)),
        ],
        compiler_params=small,
        name="attention_partials",
    )(*in_hbm(seq_lengths, block_table, query, keys, values))

    def call(kernel, out_shape, name, *operands):
        return pl.pallas_call(
            kernel,
            out_shape=out_shape,
            in_specs=[VMEM] * len(operands),
            out_specs=jax.tree.map(lambda _: VMEM, out_shape),
            compiler_params=small,
            name=name,
        )(*operands)

    def ring(x):
        one, three, two = (
            lax.ppermute(
                x,
                ("core", "tp"),
                [
                    (core * tp_size + i, (1 - core) * tp_size + (i - distance) % tp_size)
                    for core in range(2)
                    for i in range(tp_size)
                ],
            )
            for distance in (1, 3, 2)
        )
        return one, two, three

    swap = [(0, 1), (1, 0)]
    block = call(
        merge_cores_kernel, packed, "merge_cores", keep, lax.ppermute(send, "core", swap)
    )
    blocks = lax.all_to_all(block, "chip", 0, 0, tiled=True)
    finished = call(
        merge_chips_kernel,
        jax.ShapeDtypeStruct((half, rows, width), BF16),
        "merge_chips",
        blocks,
    )
    around = ring(finished)
    gate, res, gain = load(
        finished, gate_weight, residual, norm_gain.reshape(devices, width)
    )
    mine = call(
        join_kernel,
        jax.ShapeDtypeStruct((tp_size, half, rows, width), BF16),
        "join_heads",
        finished,
        *around,
        gain,
    )
    theirs = lax.ppermute(mine, "core", swap)
    mixed, share = pl.pallas_call(
        feed_kernel,
        out_shape=[
            jax.ShapeDtypeStruct((devices, rows, width), BF16),
            jax.ShapeDtypeStruct((rows, width), F32),
        ],
        in_specs=[VMEM] * 5 + [HBM] * 2,
        out_specs=[VMEM] * 2,
        scratch_shapes=[
            pltpu.VMEM(up_weight.shape, BF16),
            pltpu.VMEM(down_weight.shape, BF16),
            pltpu.VMEM((devices, rows, width), F32),
            pltpu.VMEM((rows, devices * width), BF16),
            pltpu.SemaphoreType.DMA((2, IN_STEPS)),
        ],
        compiler_params=pltpu.CompilerParams(vmem_limit_bytes=32 * MIB),
        name="feed_forward",
    )(
        mine,
        theirs,
        res,
        gain,
        gate,
        *in_hbm(up_weight, down_weight),
    )
    sums = lax.all_to_all(mixed, ("chip", "core", "tp"), 0, 0, tiled=True)
    return call(
        final_kernel,
        [jax.ShapeDtypeStruct((rows, width), BF16), jax.ShapeDtypeStruct(query.shape, BF16)],
        "add_shares",
        sums,
        share,
        finished,
        theirs,
    )


def solution(mesh):
    devices = mesh.devices
    split = Mesh(devices.reshape(-1, 2, devices.shape[1]), ("chip", "core", "tp"))
    kv = ("chip", "core")
    every = ("chip", "core", "tp")
    placed = (
        P(None, "tp", None),
        P(kv, None, "tp", None),
        P(kv, None, "tp", None),
        P(),
        P(None, kv),
        P(),
        P(),
        P(every, None),
        P(every, None),
        P(every, None),
    )
    return jax.shard_map(
        shards,
        mesh=split,
        in_specs=placed,
        out_specs=(P(None, every), P(None, "tp", None)),
        check_vma=False,
    )
```

```python
import functools

import jax
import jax.numpy as jnp
from jax import lax
from jax.experimental import pallas as pl
from jax.experimental.pallas import tpu as pltpu
from jax.sharding import Mesh
from jax.sharding import PartitionSpec as P

NEG = -1e30
F32 = jnp.float32
BF16 = jnp.bfloat16
MIB = 1 << 20
NT = (((1,), (1,)), ((), ()))
PAGES_PER_DOT = 8
PARTS = 8
CHUNK = 2048
IN_STEPS = 8
OUT_STEPS = 4
UP_HELD = 2


def kv_index():
    return lax.axis_index("chip") * lax.axis_size("core") + lax.axis_index("core")


def attention_kernel(
    lengths_h, table_h, query_h, keys, values, keep, send, lengths, table, query, k_vmem, v_vmem, sems
):
    rows, heads, width = query.shape
    pages = table.shape[1]
    cells = keys.shape[0] // (rows * pages)
    small = [
        pltpu.make_async_copy(table_h, table, sems.at[0]),
        pltpu.make_async_copy(lengths_h, lengths, sems.at[1]),
        pltpu.make_async_copy(query_h, query, sems.at[2]),
    ]
    part = keys.shape[0] // PARTS
    k_copies, v_copies = [], []
    for i in range(PARTS):
        at = pl.ds(i * part, part)
        k_copies.append(pltpu.make_async_copy(keys.at[at], k_vmem.at[at], sems.at[3 + i]))
        v_copies.append(pltpu.make_async_copy(values.at[at], v_vmem.at[at], sems.at[3 + PARTS + i]))
    for copy in small + k_copies + v_copies:
        copy.start()
    first = kv_index() * (pages * cells // 2)
    span = pages * cells
    column = lax.broadcasted_iota(jnp.int32, (heads, span), 1)
    head = lax.broadcasted_iota(jnp.int32, (heads, span), 0)
    own = (column % 2) == (head // (heads // 2))
    position = jnp.where(own, first + column // 2, jnp.int32(2**30))
    lane = lax.broadcasted_iota(jnp.int32, (heads, width), 1)
    half = heads // 2
    core = lax.axis_index("core")

    def put(row, block):
        low, high = block[:half], block[half:]
        keep[:, row, :] = jnp.where(core == 0, low, high)
        send[:, row, :] = jnp.where(core == 0, high, low)

    def block(ref, row, at):
        return jnp.concatenate(
            [
                ref[pl.ds(pl.multiple_of(table[row, at + i] * cells, cells), cells), :]
                for i in range(PAGES_PER_DOT)
            ],
            axis=0,
        )

    kept = []
    for copy in small + k_copies:
        copy.wait()
    for row in range(rows):
        q = query[row]
        scores = jnp.concatenate(
            [
                lax.dot_general(q, block(k_vmem, row, at), NT, preferred_element_type=F32)
                for at in range(0, pages, PAGES_PER_DOT)
            ],
            axis=1,
        ) * (width**-0.5)
        active = position < lengths[row]
        masked = jnp.where(active, scores, NEG)
        top = jnp.max(masked, axis=-1, keepdims=True)
        weights = jnp.where(active, jnp.exp(masked - top), 0.0)
        total = jnp.sum(weights, axis=-1, keepdims=True)
        kept.append(weights.astype(BF16))
        put(rows + row, jnp.where(lane < width // 2, top, total))
    for copy in v_copies:
        copy.wait()
    for row in range(rows):
        summed = jnp.zeros((heads, width), F32)
        for at in range(0, pages, PAGES_PER_DOT):
            summed += jnp.dot(
                kept[row][:, at * cells : (at + PAGES_PER_DOT) * cells],
                block(v_vmem, row, at),
                preferred_element_type=F32,
            )
        put(row, summed)


def pack(out, means, log_total):
    heads = len(means)
    copies = out.shape[0]
    for h in range(heads):
        mean = means[h].astype(BF16)
        for i in range(copies):
            out[i, h] = mean
    first = log_total.astype(BF16).astype(F32)
    second = (log_total - first).astype(BF16).astype(F32)
    third = log_total - first - second
    rest = jnp.zeros((first.shape[0], out.shape[-1] - 3 * heads), F32)
    terms = jnp.concatenate([first, second, third, rest], axis=1).astype(BF16)
    for i in range(copies):
        out[i, heads] = terms


def merge_cores_kernel(keep, received, loaded, out):
    heads, double, width = keep.shape
    rows = double // 2
    mine, theirs = keep[...], received[...]

    def stats(block):
        return block[:, rows:, 0:1], block[:, rows:, width // 2 : width // 2 + 1]

    top_a, total_a = stats(mine)
    top_b, total_b = stats(theirs)
    top = jnp.maximum(top_a, top_b)
    factor_a, factor_b = jnp.exp(top_a - top), jnp.exp(top_b - top)
    total = factor_a * total_a + factor_b * total_b
    summed = factor_a * mine[:, :rows, :] + factor_b * theirs[:, :rows, :]
    live = total > 0.0
    safe = jnp.where(live, total, 1.0)
    mean = jnp.where(live, summed / safe, 0.0)
    log_total = jnp.where(live, top + jnp.log(safe), NEG)
    shape = (heads, rows, width)
    here = lax.broadcasted_iota(jnp.int32, shape, 2) == lax.broadcasted_iota(jnp.int32, shape, 0)
    pack(out, list(mean), jnp.sum(jnp.where(here, log_total, 0.0), axis=0)[:, :heads])


def merge_chips_kernel(parts, out):
    count = parts.shape[0]
    heads = parts.shape[1] - 1
    logs = []
    for i in range(count):
        terms = parts[i, heads].astype(F32)
        logs.append(terms[:, :heads] + terms[:, heads : 2 * heads] + terms[:, 2 * heads : 3 * heads])
    top = functools.reduce(jnp.maximum, logs)
    factors = [jnp.exp(log - top) for log in logs]
    total = functools.reduce(jnp.add, factors)
    shares = [factor / total for factor in factors]
    for h in range(heads):
        out[h] = functools.reduce(
            jnp.add, [shares[i][:, h : h + 1] * parts[i, h].astype(F32) for i in range(count)]
        ).astype(BF16)


def join_kernel(*refs):
    for i in range(refs[-1].shape[0]):
        refs[-1][i] = refs[i][...]


def feed_kernel(
    mine,
    theirs,
    residual,
    gain,
    gate_w,
    up_first,
    up_h,
    down_h,
    out,
    share_out,
    up_w,
    down_w,
    hidden,
    normed,
    sems,
):
    groups, half, rows, width = mine.shape
    count = groups * half * 2
    features = count * width
    kv, tp = kv_index(), lax.axis_index("tp")
    in_step = features // IN_STEPS
    out_step = features // OUT_STEPS

    def pieces(source, target, which, first, steps):
        step = features // steps
        copies = []
        for i in range(first, steps):
            at = pl.ds(i * step, step)
            copies.append(
                pltpu.make_async_copy(source.at[:, at], target.at[:, at], sems.at[which, i])
            )
        return copies

    up_copies = pieces(up_h, up_w, 0, UP_HELD, IN_STEPS)
    down_copies = pieces(down_h, down_w, 1, 0, OUT_STEPS)
    for copy in up_copies + down_copies:
        copy.start()
    squares = jnp.zeros((rows, width), F32)
    for part, core in ((mine, kv % 2), (theirs, 1 - kv % 2)):
        for distance in range(groups):
            held = core if distance == 0 else 1 - core
            base = ((tp + distance) % groups) * (2 * half) + held * half
            for i in range(half):
                cols = pl.ds(pl.multiple_of((base + i) * width, width), width)
                value = residual[:, cols].astype(F32) + part[distance, i].astype(F32)
                hidden[base + i] = value
                squares += value * value
    mean_square = jnp.sum(squares, axis=-1, keepdims=True) / features
    scale = lax.rsqrt(mean_square + 1e-05)
    for i in range(count):
        cols = slice(i * width, (i + 1) * width)
        normed[:, cols] = (hidden[i] * scale * gain[i : i + 1, :].astype(F32)).astype(BF16)
    share_out[...] = hidden[kv * groups + tp]
    units = gate_w.shape[0]
    gate = jnp.zeros((rows, units), F32)
    up = jnp.zeros((rows, units), F32)
    for i in range(IN_STEPS):
        at = i * in_step
        x = normed[:, at : at + in_step]
        if i >= UP_HELD:
            up_copies[i - UP_HELD].wait()
        up_block = (up_first if i < UP_HELD else up_w)[:, at : at + in_step]
        gate += lax.dot_general(x, gate_w[:, at : at + in_step], NT, preferred_element_type=F32)
        up += lax.dot_general(x, up_block, NT, preferred_element_type=F32)
    activated = (gate / (1.0 + jnp.exp(-gate)) * up).astype(BF16)
    for i in range(OUT_STEPS):
        at = i * out_step
        down_copies[i].wait()
        for half in range(at, at + out_step, CHUNK):
            mixed = jnp.dot(activated, down_w[:, half : half + CHUNK], preferred_element_type=F32)
            for j in range(CHUNK // width):
                out[half // width + j] = mixed[:, j * width : (j + 1) * width].astype(BF16)


def load_kernel(ranges, after, *refs):
    count = len(ranges)
    sems = refs[2 * count]
    copies = []
    for i, (first, last) in enumerate(ranges):
        source = refs[i].at[:, pl.ds(first, last - first)]
        copies.append(pltpu.make_async_copy(source, refs[count + i], sems.at[i]))
    for copy in copies:
        copy.start()
    for copy in copies:
        copy.wait()


def load(after, *parts):
    arrays = [array for array, _, _ in parts]
    ranges = [(first, last) for _, first, last in parts]
    shapes = [(array.shape[0], last - first) for array, first, last in parts]
    moved = sum(2 * shape[0] * shape[1] for shape in shapes)
    return pl.pallas_call(
        functools.partial(load_kernel, ranges),
        out_shape=[pltpu.VMEM(shape, BF16) for shape in shapes],
        in_specs=[VMEM] + [HBM] * len(parts),
        out_specs=[VMEM] * len(parts),
        scratch_shapes=[pltpu.SemaphoreType.DMA((len(parts),))],
        compiler_params=pltpu.CompilerParams(vmem_limit_bytes=16 * MIB),
        cost_estimate=pl.CostEstimate(flops=0, bytes_accessed=moved, transcendentals=0),
        name="load_weights",
    )(after, *in_hbm(*arrays))


def final_kernel(parts, share, finished, theirs, layer_out, attention):
    half, rows, width = finished.shape
    first = lax.axis_index("core") == 0
    mine, other = finished[...].astype(F32), theirs[0].astype(F32)
    low = jnp.where(first, mine, other)
    high = jnp.where(first, other, mine)
    for row in range(rows):
        attention[row, :half] = low[:, row, :].astype(BF16)
        attention[row, half:] = high[:, row, :].astype(BF16)
    terms = [parts[i].astype(F32) for i in range(parts.shape[0])]
    while len(terms) > 1:
        terms = [terms[i] + terms[i + 1] for i in range(0, len(terms), 2)]
    layer_out[...] = (share[...] + terms[0]).astype(BF16)


VMEM = pl.BlockSpec(memory_space=pltpu.VMEM)
HBM = pl.BlockSpec(memory_space=pltpu.HBM)


def in_hbm(*arrays):
    return [pltpu.with_memory_space_constraint(x, pltpu.HBM) for x in arrays]


def shards(
    query,
    key_cache,
    value_cache,
    seq_lengths,
    block_table,
    residual,
    norm_gain,
    gate_weight,
    up_weight,
    down_weight,
):
    rows, heads, width = query.shape
    keys = key_cache.reshape(-1, width)
    values = value_cache.reshape(-1, width)
    kv_size, tp_size = lax.axis_size("chip") * lax.axis_size("core"), lax.axis_size("tp")
    devices = kv_size * tp_size
    half = heads // 2
    small = pltpu.CompilerParams(vmem_limit_bytes=16 * MIB)
    block_f32 = jax.ShapeDtypeStruct((half, 2 * rows, width), F32)
    packed = jax.ShapeDtypeStruct((lax.axis_size("chip"), half + 1, rows, width), BF16)
    keep, send = pl.pallas_call(
        attention_kernel,
        out_shape=[block_f32] * 2,
        in_specs=[HBM] * 5,
        out_specs=[VMEM] * 2,
        scratch_shapes=[
            pltpu.SMEM(seq_lengths.shape, jnp.int32),
            pltpu.SMEM(block_table.shape, jnp.int32),
            pltpu.VMEM(query.shape, BF16),
            pltpu.VMEM(keys.shape, BF16),
            pltpu.VMEM(values.shape, BF16),
            pltpu.SemaphoreType.DMA((3 + 2 * PARTS,)),
        ],
        compiler_params=small,
        name="attention_partials",
    )(*in_hbm(seq_lengths, block_table, query, keys, values))

    def call(kernel, out_shape, name, *operands):
        return pl.pallas_call(
            kernel,
            out_shape=out_shape,
            in_specs=[VMEM] * len(operands),
            out_specs=jax.tree.map(lambda _: VMEM, out_shape),
            compiler_params=small,
            name=name,
        )(*operands)

    def ring(x):
        one, three, two = (
            lax.ppermute(
                x,
                ("core", "tp"),
                [
                    (core * tp_size + i, (1 - core) * tp_size + (i - distance) % tp_size)
                    for core in range(2)
                    for i in range(tp_size)
                ],
            )
            for distance in (1, 3, 2)
        )
        return one, two, three

    swap = [(0, 1), (1, 0)]
    received = lax.ppermute(send, "core", swap)
    features = residual.shape[1]
    (up_first,) = load(keep, (up_weight, 0, UP_HELD * (features // IN_STEPS)))
    block = call(merge_cores_kernel, packed, "merge_cores", keep, received, up_first)
    blocks = lax.all_to_all(block, "chip", 0, 0, tiled=True)
    finished = call(
        merge_chips_kernel,
        jax.ShapeDtypeStruct((half, rows, width), BF16),
        "merge_chips",
        blocks,
    )
    around = ring(finished)
    gains = norm_gain.reshape(devices, width)
    gate, res, gain = load(
        finished, (gate_weight, 0, features), (residual, 0, features), (gains, 0, width)
    )
    mine = call(
        join_kernel,
        jax.ShapeDtypeStruct((tp_size, half, rows, width), BF16),
        "join_heads",
        finished,
        *around,
        gain,
    )
    theirs = lax.ppermute(mine, "core", swap)
    mixed, share = pl.pallas_call(
        feed_kernel,
        out_shape=[
            jax.ShapeDtypeStruct((devices, rows, width), BF16),
            jax.ShapeDtypeStruct((rows, width), F32),
        ],
        in_specs=[VMEM] * 6 + [HBM] * 2,
        out_specs=[VMEM] * 2,
        scratch_shapes=[
            pltpu.VMEM(up_weight.shape, BF16),
            pltpu.VMEM(down_weight.shape, BF16),
            pltpu.VMEM((devices, rows, width), F32),
            pltpu.VMEM((rows, devices * width), BF16),
            pltpu.SemaphoreType.DMA((2, IN_STEPS)),
        ],
        compiler_params=pltpu.CompilerParams(vmem_limit_bytes=32 * MIB),
        name="feed_forward",
    )(
        mine,
        theirs,
        res,
        gain,
        gate,
        up_first,
        *in_hbm(up_weight, down_weight),
    )
    sums = lax.all_to_all(mixed, ("chip", "core", "tp"), 0, 0, tiled=True)
    return call(
        final_kernel,
        [jax.ShapeDtypeStruct((rows, width), BF16), jax.ShapeDtypeStruct(query.shape, BF16)],
        "add_shares",
        sums,
        share,
        finished,
        theirs,
    )


def solution(mesh):
    devices = mesh.devices
    split = Mesh(devices.reshape(-1, 2, devices.shape[1]), ("chip", "core", "tp"))
    kv = ("chip", "core")
    every = ("chip", "core", "tp")
    placed = (
        P(None, "tp", None),
        P(kv, None, "tp", None),
        P(kv, None, "tp", None),
        P(),
        P(None, kv),
        P(),
        P(),
        P(every, None),
        P(every, None),
        P(every, None),
    )
    return jax.shard_map(
        shards,
        mesh=split,
        in_specs=placed,
        out_specs=(P(None, every), P(None, "tp", None)),
        check_vma=False,
    )
```

```python
import functools

import jax
import jax.numpy as jnp
from jax import lax
from jax.experimental import pallas as pl
from jax.experimental.pallas import tpu as pltpu
from jax.sharding import Mesh
from jax.sharding import PartitionSpec as P

NEG = -1e30
F32 = jnp.float32
BF16 = jnp.bfloat16
MIB = 1 << 20
NT = (((1,), (1,)), ((), ()))
PAGES_PER_DOT = 8
PARTS = 8
CHUNK = 2048
IN_STEPS = 8
OUT_STEPS = 4
UP_HELD = 1


def kv_index():
    return lax.axis_index("chip") * lax.axis_size("core") + lax.axis_index("core")


def attention_kernel(
    lengths_h, table_h, query_h, keys, values, keep, send, lengths, table, query, k_vmem, v_vmem, sems
):
    rows, heads, width = query.shape
    pages = table.shape[1]
    cells = keys.shape[0] // (rows * pages)
    small = [
        pltpu.make_async_copy(table_h, table, sems.at[0]),
        pltpu.make_async_copy(lengths_h, lengths, sems.at[1]),
        pltpu.make_async_copy(query_h, query, sems.at[2]),
    ]
    part = keys.shape[0] // PARTS
    k_copies, v_copies = [], []
    for i in range(PARTS):
        at = pl.ds(i * part, part)
        k_copies.append(pltpu.make_async_copy(keys.at[at], k_vmem.at[at], sems.at[3 + i]))
        v_copies.append(pltpu.make_async_copy(values.at[at], v_vmem.at[at], sems.at[3 + PARTS + i]))
    for copy in small + k_copies + v_copies:
        copy.start()
    first = kv_index() * (pages * cells // 2)
    span = pages * cells
    column = lax.broadcasted_iota(jnp.int32, (heads, span), 1)
    head = lax.broadcasted_iota(jnp.int32, (heads, span), 0)
    own = (column % 2) == (head // (heads // 2))
    position = jnp.where(own, first + column // 2, jnp.int32(2**30))
    lane = lax.broadcasted_iota(jnp.int32, (heads, width), 1)
    half = heads // 2
    core = lax.axis_index("core")

    def put(row, block):
        low, high = block[:half], block[half:]
        keep[:, row, :] = jnp.where(core == 0, low, high)
        send[:, row, :] = jnp.where(core == 0, high, low)

    def block(ref, row, at):
        return jnp.concatenate(
            [
                ref[pl.ds(pl.multiple_of(table[row, at + i] * cells, cells), cells), :]
                for i in range(PAGES_PER_DOT)
            ],
            axis=0,
        )

    kept = []
    for copy in small + k_copies:
        copy.wait()
    for row in range(rows):
        q = query[row]
        scores = jnp.concatenate(
            [
                lax.dot_general(q, block(k_vmem, row, at), NT, preferred_element_type=F32)
                for at in range(0, pages, PAGES_PER_DOT)
            ],
            axis=1,
        ) * (width**-0.5)
        active = position < lengths[row]
        masked = jnp.where(active, scores, NEG)
        top = jnp.max(masked, axis=-1, keepdims=True)
        weights = jnp.where(active, jnp.exp(masked - top), 0.0)
        total = jnp.sum(weights, axis=-1, keepdims=True)
        kept.append(weights.astype(BF16))
        put(rows + row, jnp.where(lane < width // 2, top, total))
    for copy in v_copies:
        copy.wait()
    for row in range(rows):
        summed = jnp.zeros((heads, width), F32)
        for at in range(0, pages, PAGES_PER_DOT):
            summed += jnp.dot(
                kept[row][:, at * cells : (at + PAGES_PER_DOT) * cells],
                block(v_vmem, row, at),
                preferred_element_type=F32,
            )
        put(row, summed)


def pack(out, means, log_total):
    heads = len(means)
    copies = out.shape[0]
    for h in range(heads):
        mean = means[h].astype(BF16)
        for i in range(copies):
            out[i, h] = mean
    first = log_total.astype(BF16).astype(F32)
    second = (log_total - first).astype(BF16).astype(F32)
    third = log_total - first - second
    rest = jnp.zeros((first.shape[0], out.shape[-1] - 3 * heads), F32)
    terms = jnp.concatenate([first, second, third, rest], axis=1).astype(BF16)
    for i in range(copies):
        out[i, heads] = terms


def merge_cores_kernel(keep, received, loaded, out):
    heads, double, width = keep.shape
    rows = double // 2
    mine, theirs = keep[...], received[...]

    def stats(block):
        return block[:, rows:, 0:1], block[:, rows:, width // 2 : width // 2 + 1]

    top_a, total_a = stats(mine)
    top_b, total_b = stats(theirs)
    top = jnp.maximum(top_a, top_b)
    factor_a, factor_b = jnp.exp(top_a - top), jnp.exp(top_b - top)
    total = factor_a * total_a + factor_b * total_b
    summed = factor_a * mine[:, :rows, :] + factor_b * theirs[:, :rows, :]
    live = total > 0.0
    safe = jnp.where(live, total, 1.0)
    mean = jnp.where(live, summed / safe, 0.0)
    log_total = jnp.where(live, top + jnp.log(safe), NEG)
    shape = (heads, rows, width)
    here = lax.broadcasted_iota(jnp.int32, shape, 2) == lax.broadcasted_iota(jnp.int32, shape, 0)
    pack(out, list(mean), jnp.sum(jnp.where(here, log_total, 0.0), axis=0)[:, :heads])


def merge_chips_kernel(parts, out):
    count = parts.shape[0]
    heads = parts.shape[1] - 1
    logs = []
    for i in range(count):
        terms = parts[i, heads].astype(F32)
        logs.append(terms[:, :heads] + terms[:, heads : 2 * heads] + terms[:, 2 * heads : 3 * heads])
    top = functools.reduce(jnp.maximum, logs)
    factors = [jnp.exp(log - top) for log in logs]
    total = functools.reduce(jnp.add, factors)
    shares = [factor / total for factor in factors]
    for h in range(heads):
        out[h] = functools.reduce(
            jnp.add, [shares[i][:, h : h + 1] * parts[i, h].astype(F32) for i in range(count)]
        ).astype(BF16)


def join_kernel(*refs):
    for i in range(refs[-1].shape[0]):
        refs[-1][i] = refs[i][...]


def feed_kernel(
    mine,
    theirs,
    residual,
    gain,
    gate_w,
    up_first,
    up_h,
    down_h,
    out,
    share_out,
    up_w,
    down_w,
    hidden,
    normed,
    sems,
):
    groups, half, rows, width = mine.shape
    count = groups * half * 2
    features = count * width
    kv, tp = kv_index(), lax.axis_index("tp")
    in_step = features // IN_STEPS
    out_step = features // OUT_STEPS

    def pieces(source, target, which, first, steps):
        step = features // steps
        copies = []
        for i in range(first, steps):
            at = pl.ds(i * step, step)
            copies.append(
                pltpu.make_async_copy(source.at[:, at], target.at[:, at], sems.at[which, i])
            )
        return copies

    up_copies = pieces(up_h, up_w, 0, UP_HELD, IN_STEPS)
    down_copies = pieces(down_h, down_w, 1, 0, OUT_STEPS)
    for copy in up_copies + down_copies:
        copy.start()
    squares = jnp.zeros((rows, width), F32)
    for part, core in ((mine, kv % 2), (theirs, 1 - kv % 2)):
        for distance in range(groups):
            held = core if distance == 0 else 1 - core
            base = ((tp + distance) % groups) * (2 * half) + held * half
            for i in range(half):
                cols = pl.ds(pl.multiple_of((base + i) * width, width), width)
                value = residual[:, cols].astype(F32) + part[distance, i].astype(F32)
                hidden[base + i] = value
                squares += value * value
    mean_square = jnp.sum(squares, axis=-1, keepdims=True) / features
    scale = lax.rsqrt(mean_square + 1e-05)
    for i in range(count):
        cols = slice(i * width, (i + 1) * width)
        normed[:, cols] = (hidden[i] * scale * gain[i : i + 1, :].astype(F32)).astype(BF16)
    share_out[...] = hidden[kv * groups + tp]
    units = gate_w.shape[0]
    gate = jnp.zeros((rows, units), F32)
    up = jnp.zeros((rows, units), F32)
    for i in range(IN_STEPS):
        at = i * in_step
        x = normed[:, at : at + in_step]
        if i >= UP_HELD:
            up_copies[i - UP_HELD].wait()
        up_block = (up_first if i < UP_HELD else up_w)[:, at : at + in_step]
        gate += lax.dot_general(x, gate_w[:, at : at + in_step], NT, preferred_element_type=F32)
        up += lax.dot_general(x, up_block, NT, preferred_element_type=F32)
    activated = (gate / (1.0 + jnp.exp(-gate)) * up).astype(BF16)
    for i in range(OUT_STEPS):
        at = i * out_step
        down_copies[i].wait()
        for half in range(at, at + out_step, CHUNK):
            mixed = jnp.dot(activated, down_w[:, half : half + CHUNK], preferred_element_type=F32)
            for j in range(CHUNK // width):
                out[half // width + j] = mixed[:, j * width : (j + 1) * width].astype(BF16)


def load_kernel(ranges, after, *refs):
    count = len(ranges)
    sems = refs[2 * count]
    copies = []
    for i, (first, last) in enumerate(ranges):
        source = refs[i].at[:, pl.ds(first, last - first)]
        copies.append(pltpu.make_async_copy(source, refs[count + i], sems.at[i]))
    for copy in copies:
        copy.start()
    for copy in copies:
        copy.wait()


def load(after, *parts):
    arrays = [array for array, _, _ in parts]
    ranges = [(first, last) for _, first, last in parts]
    shapes = [(array.shape[0], last - first) for array, first, last in parts]
    moved = sum(2 * shape[0] * shape[1] for shape in shapes)
    return pl.pallas_call(
        functools.partial(load_kernel, ranges),
        out_shape=[pltpu.VMEM(shape, BF16) for shape in shapes],
        in_specs=[VMEM] + [HBM] * len(parts),
        out_specs=[VMEM] * len(parts),
        scratch_shapes=[pltpu.SemaphoreType.DMA((len(parts),))],
        compiler_params=pltpu.CompilerParams(vmem_limit_bytes=16 * MIB),
        cost_estimate=pl.CostEstimate(flops=0, bytes_accessed=moved, transcendentals=0),
        name="load_weights",
    )(after, *in_hbm(*arrays))


def final_kernel(parts, share, finished, theirs, layer_out, attention):
    half, rows, width = finished.shape
    first = lax.axis_index("core") == 0
    mine, other = finished[...].astype(F32), theirs[0].astype(F32)
    low = jnp.where(first, mine, other)
    high = jnp.where(first, other, mine)
    for row in range(rows):
        attention[row, :half] = low[:, row, :].astype(BF16)
        attention[row, half:] = high[:, row, :].astype(BF16)
    terms = [parts[i].astype(F32) for i in range(parts.shape[0])]
    while len(terms) > 1:
        terms = [terms[i] + terms[i + 1] for i in range(0, len(terms), 2)]
    layer_out[...] = (share[...] + terms[0]).astype(BF16)


VMEM = pl.BlockSpec(memory_space=pltpu.VMEM)
HBM = pl.BlockSpec(memory_space=pltpu.HBM)


def in_hbm(*arrays):
    return [pltpu.with_memory_space_constraint(x, pltpu.HBM) for x in arrays]


def shards(
    query,
    key_cache,
    value_cache,
    seq_lengths,
    block_table,
    residual,
    norm_gain,
    gate_weight,
    up_weight,
    down_weight,
):
    rows, heads, width = query.shape
    keys = key_cache.reshape(-1, width)
    values = value_cache.reshape(-1, width)
    kv_size, tp_size = lax.axis_size("chip") * lax.axis_size("core"), lax.axis_size("tp")
    devices = kv_size * tp_size
    half = heads // 2
    small = pltpu.CompilerParams(vmem_limit_bytes=16 * MIB)
    block_f32 = jax.ShapeDtypeStruct((half, 2 * rows, width), F32)
    packed = jax.ShapeDtypeStruct((lax.axis_size("chip"), half + 1, rows, width), BF16)
    keep, send = pl.pallas_call(
        attention_kernel,
        out_shape=[block_f32] * 2,
        in_specs=[HBM] * 5,
        out_specs=[VMEM] * 2,
        scratch_shapes=[
            pltpu.SMEM(seq_lengths.shape, jnp.int32),
            pltpu.SMEM(block_table.shape, jnp.int32),
            pltpu.VMEM(query.shape, BF16),
            pltpu.VMEM(keys.shape, BF16),
            pltpu.VMEM(values.shape, BF16),
            pltpu.SemaphoreType.DMA((3 + 2 * PARTS,)),
        ],
        compiler_params=small,
        name="attention_partials",
    )(*in_hbm(seq_lengths, block_table, query, keys, values))

    def call(kernel, out_shape, name, *operands):
        return pl.pallas_call(
            kernel,
            out_shape=out_shape,
            in_specs=[VMEM] * len(operands),
            out_specs=jax.tree.map(lambda _: VMEM, out_shape),
            compiler_params=small,
            name=name,
        )(*operands)

    def ring(x):
        one, three, two = (
            lax.ppermute(
                x,
                ("core", "tp"),
                [
                    (core * tp_size + i, (1 - core) * tp_size + (i - distance) % tp_size)
                    for core in range(2)
                    for i in range(tp_size)
                ],
            )
            for distance in (1, 3, 2)
        )
        return one, two, three

    swap = [(0, 1), (1, 0)]
    received = lax.ppermute(send, "core", swap)
    features = residual.shape[1]
    (up_first,) = load(keep, (up_weight, 0, UP_HELD * (features // IN_STEPS)))
    block = call(merge_cores_kernel, packed, "merge_cores", keep, received, up_first)
    blocks = lax.all_to_all(block, "chip", 0, 0, tiled=True)
    finished = call(
        merge_chips_kernel,
        jax.ShapeDtypeStruct((half, rows, width), BF16),
        "merge_chips",
        blocks,
    )
    around = ring(finished)
    gains = norm_gain.reshape(devices, width)
    gate, res, gain = load(
        finished, (gate_weight, 0, features), (residual, 0, features), (gains, 0, width)
    )
    mine = call(
        join_kernel,
        jax.ShapeDtypeStruct((tp_size, half, rows, width), BF16),
        "join_heads",
        finished,
        *around,
        gain,
    )
    theirs = lax.ppermute(mine, "core", swap)
    mixed, share = pl.pallas_call(
        feed_kernel,
        out_shape=[
            jax.ShapeDtypeStruct((devices, rows, width), BF16),
            jax.ShapeDtypeStruct((rows, width), F32),
        ],
        in_specs=[VMEM] * 6 + [HBM] * 2,
        out_specs=[VMEM] * 2,
        scratch_shapes=[
            pltpu.VMEM(up_weight.shape, BF16),
            pltpu.VMEM(down_weight.shape, BF16),
            pltpu.VMEM((devices, rows, width), F32),
            pltpu.VMEM((rows, devices * width), BF16),
            pltpu.SemaphoreType.DMA((2, IN_STEPS)),
        ],
        compiler_params=pltpu.CompilerParams(vmem_limit_bytes=32 * MIB),
        name="feed_forward",
    )(
        mine,
        theirs,
        res,
        gain,
        gate,
        up_first,
        *in_hbm(up_weight, down_weight),
    )
    sums = lax.all_to_all(mixed, ("chip", "core", "tp"), 0, 0, tiled=True)
    return call(
        final_kernel,
        [jax.ShapeDtypeStruct((rows, width), BF16), jax.ShapeDtypeStruct(query.shape, BF16)],
        "add_shares",
        sums,
        share,
        finished,
        theirs,
    )


def solution(mesh):
    devices = mesh.devices
    split = Mesh(devices.reshape(-1, 2, devices.shape[1]), ("chip", "core", "tp"))
    kv = ("chip", "core")
    every = ("chip", "core", "tp")
    placed = (
        P(None, "tp", None),
        P(kv, None, "tp", None),
        P(kv, None, "tp", None),
        P(),
        P(None, kv),
        P(),
        P(),
        P(every, None),
        P(every, None),
        P(every, None),
    )
    return jax.shard_map(
        shards,
        mesh=split,
        in_specs=placed,
        out_specs=(P(None, every), P(None, "tp", None)),
        check_vma=False,
    )
```
